256 devices in a mesh: gx: 8 (over y, x_hi), gy: 4 (over x_lo, core), gz: 8 (over z).
Axes of the slice: x: 4 (x_hi: 2, x_lo: 2; x = x_hi * 2 + x_lo), y: 4, z: 8, core: 2. Of those that a mesh axis runs over, the one named last changes fastest.
Arguments:
- features: bfloat16 [32, 128, 64, 1024], P(None, ('gx', 'gy'), None, 'gz'), may hold values from -6 to 6
- conv_weight: bfloat16 [32, 27], replicated, may hold values from -0.21875 to 0.21875
- weight_step: bfloat16 [32, 27], replicated, may hold values from -0.21875 to 0.21875
- conv_bias: float32 [1], replicated, may hold values from -0.5 to 0.5
- wave_state: float32 [2, 2, 128, 64, 1024], P(None, None, ('gx', 'gy'), None, 'gz'), may hold values from -6 to 6
- born_in: float32 [2, 2, 128, 64, 1024], P(None, None, ('gx', 'gy'), None, 'gz'), may hold values from -6 to 6
- adjoint_in: float32 [2, 2, 128, 64, 1024], P(None, None, ('gx', 'gy'), None, 'gz'), may hold values from -6 to 6
- shot_x: int32 [2], replicated, may hold values from 0 to 127, as said below
- shot_y: int32 [2], replicated, may hold values from 0 to 63, as said below
- rec_x: int32 [1024], replicated, may hold values from 0 to 127
- rec_y: int32 [1024], replicated, may hold values from 0 to 63
Outputs:
- born_state: float32 [2, 2, 128, 64, 1024], P(None, None, ('gx', 'gy'), None, 'gz')
- adjoint_state: float32 [2, 2, 128, 64, 1024], P(None, None, ('gx', 'gy'), None, 'gz')
- weight_product: float32 [32, 27], replicated
- feature_grad: bfloat16 [32, 128, 64, 1024], P(None, ('gx', 'gy'), None, 'gz')
The draws below stay inside these ranges and needn't reach their ends.
Inputs may be any that keep to these rules, and one draw needn't show every extreme that they name: `shot_x`: shot s lies at a first index from s * (64) to (s + 1) * 64 - 1; the last shot lies at the last one. `shot_y`: shot s lies at a second index from s * (32) to (s + 1) * 32 - 1; the last shot lies at the last one.
All inputs are finite; a program needn't handle non-finite values.
Results may differ from the reference program's by a relative error of at most 0.0049.
Values may be sent and summed in bfloat16 or wider, within the bound.
A program may use at most 128 MiB of HBM per device.

```python
import math
import jax
import jax.numpy as jnp
from jax import lax

C = 32
TAPS = 27
CZ = 128
NT = 12
SHOTS = 2
NREC = 1024
SRC_DEPTH = 6
REC_DEPTH = 2
NX = 128
NY = 64
NZ = 1024


def spread_shots(key, extent):
    stretch = extent // SHOTS
    offsets = jax.random.randint(key, (SHOTS,), 0, stretch).astype(jnp.int32)
    order = jnp.arange(SHOTS).astype(jnp.int32)
    offsets = jnp.where(order == SHOTS - 1, stretch - 1, offsets).astype(jnp.int32)
    return (order * stretch + offsets).astype(jnp.int32)


def draw_shot_x(key, part):
    key = jax.random.fold_in(key, 11)
    return spread_shots(key, NX)


def draw_shot_y(key, part):
    key = jax.random.fold_in(key, 23)
    return spread_shots(key, NY)


def place_ends(values, stream_key, smallest, largest):
    shape = values.shape
    spot = [jax.random.randint(jax.random.fold_in(stream_key, axis), (), 0, shape[axis]) for axis in range(len(shape))]
    values = values.at[tuple(spot)].set(smallest)
    longest = shape.index(max(shape))
    spot[longest] = (spot[longest] + 1) % shape[longest]
    return values.at[tuple(spot)].set(largest)


def levels(rng, dims, split, least, largest):
    factor_of, own = 1.0, jax.random.fold_in(rng, 6)
    for axis_at, blocks in split:
        heights = jnp.exp(jax.random.uniform(jax.random.fold_in(own, axis_at), (blocks,), jnp.float32, least / len(split), largest / len(split)))
        factor_of = factor_of * jnp.repeat(heights, dims[axis_at] // blocks).reshape([-1 if axis == axis_at else 1 for axis in range(len(dims))])
    return factor_of


def bell_draw(stream_key, shape, width, bound, cuts=(), held_as=jnp.bfloat16):
    array = jax.random.normal(stream_key, shape, jnp.float32) * width
    if len(cuts) > 0:
        array = levels(stream_key, shape, cuts, -0.22, 0.18) * array
    return jnp.clip(array, min=-bound, max=bound).astype(held_as)


def setup_inputs(seed: int = 0) -> dict:
    keys = jax.random.split(jax.random.key(seed), 12)
    return {
        "features": bell_draw(keys[0], (C, NX, NY, NZ), 1.0, 6.0, ((1, 32), (3, 8))),
        "conv_weight": bell_draw(keys[1], (C, TAPS), (C * TAPS) ** -0.5, 0.21875),
        "weight_step": bell_draw(keys[2], (C, TAPS), (C * TAPS) ** -0.5, 0.21875),
        "conv_bias": jnp.clip(jax.random.uniform(keys[3], (1,), jnp.float32, -0.5, 0.5), -0.5, 0.5),
        "wave_state": bell_draw(keys[4], (2, SHOTS, NX, NY, NZ), 1.0, 6.0, ((2, 32), (4, 8)), jnp.float32),
        "born_in": bell_draw(keys[5], (2, SHOTS, NX, NY, NZ), 1.0, 6.0, ((2, 32), (4, 8)), jnp.float32),
        "adjoint_in": bell_draw(keys[6], (2, SHOTS, NX, NY, NZ), 1.0, 6.0, ((2, 32), (4, 8)), jnp.float32),
        "shot_x": draw_shot_x(jax.random.fold_in(keys[11], 71), 0),
        "shot_y": draw_shot_y(jax.random.fold_in(keys[11], 71), 0),
        "rec_x": place_ends(jax.random.randint(keys[9], (NREC,), 0, NX), jax.random.fold_in(keys[9], 1), 0, NX - 1).astype(jnp.int32),
        "rec_y": place_ends(jax.random.randint(keys[10], (NREC,), 0, NY), jax.random.fold_in(keys[10], 1), 0, NY - 1).astype(jnp.int32),
    }


COEFFS = (1.6, -0.2, 8.0 / 315.0, -1.0 / 560.0)
CENTER = -205.0 / 72.0
QUOTIENT = 0.0074

def stencil(extended, size_x, size_y, size_z):

    def window(shift_x, shift_y, shift_z):
        return extended[..., shift_x:shift_x + size_x, shift_y:shift_y + size_y, shift_z:shift_z + size_z]
    result = 3.0 * CENTER * window(4, 4, 4)
    for reach in range(1, 5):
        pairs = window(4 + reach, 4, 4) + window(4 - reach, 4, 4)
        pairs = pairs + window(4, 4 + reach, 4) + window(4, 4 - reach, 4)
        pairs = pairs + window(4, 4, 4 + reach) + window(4, 4, 4 - reach)
        result = result + COEFFS[reach - 1] * pairs
    return result

def laplace(field):
    size_x, size_y, size_z = field.shape[-3:]
    leading = [(0, 0)] * (field.ndim - 3)
    padded = jnp.pad(field, leading + [(4, 4)] * 3)
    return stencil(padded, size_x, size_y, size_z)

def wavelet():
    steps = jnp.arange(NT).astype(jnp.float32)
    spread = (0.45 * (steps - 5.0)) ** 2
    return 20.0 * (1.0 - 2.0 * spread) * jnp.exp(-spread)

def tap_sum(padded, weights, size_x, size_y, size_z):
    channels = padded.shape[0]
    spatial = padded.shape[1:]
    projected = jnp.dot(weights.T, padded.reshape(channels, -1), preferred_element_type=jnp.float32)
    projected = projected.reshape((weights.shape[1] // 27, 27) + spatial)
    result = jnp.zeros((weights.shape[1] // 27, size_x, size_y, size_z), jnp.float32)
    for tap_index in range(27):
        shift_x, shift_y, shift_z = (tap_index // 9, tap_index // 3 % 3, tap_index % 3)
        result = result + projected[:, tap_index, shift_x:shift_x + size_x, shift_y:shift_y + size_y, shift_z:shift_z + size_z]
    return result

def weight_moments(padded, cotangent):
    layers = []
    for tap_index in range(27):
        shift_x, shift_y, shift_z = (tap_index // 9, tap_index // 3 % 3, tap_index % 3)
        layers.append(jnp.pad(cotangent, ((shift_x, 2 - shift_x), (shift_y, 2 - shift_y), (shift_z, 2 - shift_z))))
    shifted = jnp.stack(layers).reshape(27, -1)
    return jnp.dot(padded.reshape(padded.shape[0], -1), shifted.T, preferred_element_type=jnp.float32)

def feature_cotangent(cot_padded, weights, size_x, size_y, size_z):
    layers = []
    for tap_index in range(27):
        shift_x, shift_y, shift_z = (tap_index // 9, tap_index // 3 % 3, tap_index % 3)
        layers.append(cot_padded[2 - shift_x:2 - shift_x + size_x, 2 - shift_y:2 - shift_y + size_y, 2 - shift_z:2 - shift_z + size_z])
    stacked = jnp.stack(layers).reshape(27, -1)
    product = jnp.dot(weights, stacked, preferred_element_type=jnp.float32)
    return product.reshape((weights.shape[0], size_x, size_y, size_z)).astype(jnp.bfloat16)

def reference(features, conv_weight, weight_step, conv_bias, wave_state, born_in, adjoint_in, shot_x, shot_y, rec_x, rec_y):
    padded = jnp.pad(features, ((0, 0), (1, 1), (1, 1), (1, 1)))
    stacked = jnp.concatenate([conv_weight, weight_step], axis=1)
    blocks_count = NZ // CZ
    block_ids = jnp.arange(blocks_count).astype(jnp.int32)

    def generate(block):
        sliced = lax.dynamic_slice_in_dim(padded, block * CZ, CZ + 2, axis=3)
        return tap_sum(sliced, stacked, NX, NY, CZ)
    generated = lax.map(generate, block_ids)
    both = jnp.moveaxis(generated, 0, 3).reshape((2, NX, NY, NZ))
    sigma = jax.nn.sigmoid(both[0] + conv_bias[0])
    velocity = 1.5 + 3.0 * sigma
    slope = 3.0 * sigma * (1.0 - sigma)
    velocity_step = slope * both[1]
    stiffness = QUOTIENT * velocity * velocity
    stiffness_step = 2.0 * QUOTIENT * velocity * velocity_step
    grid_x = jnp.arange(NX).astype(jnp.int32)
    grid_y = jnp.arange(NY).astype(jnp.int32)
    grid_z = jnp.arange(NZ).astype(jnp.int32)
    onehot_x = (grid_x[None, :] == shot_x[:, None]).astype(jnp.float32)
    onehot_y = (grid_y[None, :] == shot_y[:, None]).astype(jnp.float32)
    onehot_z = (grid_z == SRC_DEPTH).astype(jnp.float32)
    spot = onehot_x[:, :, None, None] * onehot_y[:, None, :, None] * onehot_z
    receive_x = (rec_x[:, None] == grid_x[None, :]).astype(jnp.float32)
    receive_y = (rec_y[:, None] == grid_y[None, :]).astype(jnp.float32)
    counts = jnp.dot(receive_x.T, receive_y, precision=lax.Precision.HIGHEST)

    def born(step_field, born_prev, born_now):

        def advance(carry, amplitude):
            wave_prev, wave_now, field_prev, field_now = carry
            drive = laplace(wave_now)
            bent = laplace(field_now)
            wave_next = 2.0 * wave_now - wave_prev + stiffness * drive + amplitude * spot
            field_next = 2.0 * field_now - field_prev + stiffness * bent + step_field * drive
            record = counts * field_next[..., REC_DEPTH]
            return ((wave_now, wave_next, field_now, field_next), record)
        final, records = lax.scan(advance, (wave_state[0], wave_state[1], born_prev, born_now), wavelet())
        return (records, final[2], final[3])
    outputs, pullback = jax.vjp(born, stiffness_step, born_in[0], born_in[1])
    records, end_prev, end_now = outputs
    step_grad, grad_prev, grad_now = pullback((records, adjoint_in[0], adjoint_in[1]))
    cotangent = (slope * (2.0 * QUOTIENT * velocity * step_grad)).astype(jnp.bfloat16)
    cot_padded = jnp.pad(cotangent, 1)

    def moments(block):
        sliced = lax.dynamic_slice_in_dim(padded, block * CZ, CZ + 2, axis=3)
        local_cot = lax.dynamic_slice_in_dim(cotangent, block * CZ, CZ, axis=2)
        return weight_moments(sliced, local_cot)
    moment_sum = lax.optimization_barrier(jnp.sum(lax.map(moments, block_ids), axis=0))
    weight_product = moment_sum / math.sqrt(NX * NY * NZ) + weight_step.astype(jnp.float32)

    def back_features(block):
        sliced = lax.dynamic_slice_in_dim(cot_padded, block * CZ, CZ + 2, axis=2)
        return feature_cotangent(sliced, conv_weight, NX, NY, CZ)
    pieces = lax.map(back_features, block_ids)
    feature_grad = jnp.moveaxis(pieces, 0, 3).reshape((C, NX, NY, NZ))
    born_state = jnp.stack([end_prev, end_now])
    adjoint_state = jnp.stack([grad_prev, grad_now])
    return (born_state, adjoint_state, weight_product, feature_grad)
```

```python
import functools
import math

import jax
import jax.numpy as jnp
import ml_dtypes
import numpy as np
from jax import lax
from jax.experimental import pallas as pl
from jax.experimental.pallas import tpu as pltpu
from jax.sharding import PartitionSpec as P

NT = 12
SRC_DEPTH = 6
REC_DEPTH = 2
QUOTIENT = 0.0074
COEFFS5 = (8.0, -1.0, 8.0 / 63.0, -1.0 / 112.0)
CENTER5 = 15.0 * (-205.0 / 72.0)

C = 32
SX = 4
NY = 64
NZ = 128
ROWS = SX * NY
CY = C * NY
MESH = pl.DeviceIdType.MESH
F32 = jnp.float32
BF16 = jnp.bfloat16
VMEM_LIMIT = 56 * 2**20


def coefficient(distance):
    out = np.zeros(distance.shape, np.float32)
    for reach in range(1, 5):
        out[distance == reach] = COEFFS5[reach - 1]
    return out


def stencil_tables():
    row = np.arange(ROWS)
    x, y = row // NY, row % NY
    dx, dy = x[:, None] - x[None, :], y[:, None] - y[None, :]
    same_x, same_y = (dx == 0), (dy == 0)
    plane = coefficient(np.abs(dx)) * same_y + coefficient(np.abs(dy)) * same_x
    plane = np.concatenate([plane, plane], axis=1)
    left = coefficient(dx + SX) * same_y
    right = coefficient(SX - dx) * same_y
    halo_x = np.concatenate([left, right], axis=1)
    z = np.arange(NZ)
    line = coefficient(np.abs(z[:, None] - z[None, :]))
    line = np.concatenate([line, line], axis=0)
    halo_z = np.zeros((32, NZ), np.float32)
    pick = np.zeros((32, NZ), np.float32)
    for k in range(4):
        halo_z[k] = coefficient(z + 4 - k)
        halo_z[16 + k] = coefficient(NZ + k - z)
        pick[k, NZ - 4 + k] = 1.0
        pick[16 + k, k] = 1.0
    return [t.astype(ml_dtypes.bfloat16) for t in (plane, halo_x, line, halo_z, pick)]


def dot(a, b):
    return jnp.dot(a, b, preferred_element_type=F32)


def dot_nt(a, b):
    return lax.dot_general(a, b, (((1,), (1,)), ((), ())), preferred_element_type=F32)


def dot_tn(a, b):
    return lax.dot_general(a, b, (((0,), (0,)), ((), ())), preferred_element_type=F32)


def split(values):
    high = values.astype(BF16)
    return high, (values - high.astype(F32)).astype(BF16)


def iota(shape, dim):
    return lax.broadcasted_iota(jnp.int32, shape, dim)


def conv_kernel(f_ref, w_ref, v_ref, planes_ref, up_ref, down_ref, band, wide):
    lane = iota((C, CY), 1)
    repeat = jnp.where(lane // NY == iota((C, CY), 0), 1.0, 0.0).astype(BF16)
    expanded = [dot_tn(w_ref[...], repeat), dot_tn(v_ref[...], repeat)]
    offset = lax.rem(iota((NY, CY), 1), NY) - iota((NY, CY), 0)
    for i in range(3):
        for l in range(3):
            for o in range(2):
                block = jnp.zeros((NY, CY), F32)
                for j in range(3):
                    tap = (i * 3 + j) * 3 + l
                    block = jnp.where(offset == j - 1, expanded[o][tap : tap + 1, :], block)
                start = ((i * 3 + l) * 2 + o) * NY
                band[start : start + NY, :] = block.astype(BF16)
    zero = jnp.zeros((CY, NZ), BF16)
    wide[:, 0:NZ] = zero
    wide[:, 5 * NZ : 6 * NZ] = zero
    for x in range(SX):
        wide[:, (x + 1) * NZ : (x + 2) * NZ] = f_ref[:, x].reshape(CY, NZ)
    z = iota((2 * NY, NZ), 1)
    pick_last = jnp.where(
        (iota((8, NZ), 1) == NZ - 1) & (iota((8, NZ), 0) == 0), 1.0, 0.0
    ).astype(BF16)
    pick_first = jnp.where(
        (iota((8, NZ), 1) == 0) & (iota((8, NZ), 0) == 0), 1.0, 0.0
    ).astype(BF16)
    for pair in range(3):
        total = jnp.zeros((6 * NY, 2 * NZ), F32)
        for i in range(3):
            first = 2 * pair + i - 1
            if first < 0 or first > 4:
                continue
            total = total + dot(
                band[i * 6 * NY : (i + 1) * 6 * NY, :], wide[:, first * NZ : (first + 2) * NZ]
            )
        for half in range(2):
            at = 2 * pair + half
            part = total[:, half * NZ : (half + 1) * NZ]
            lower, middle, upper = [part[l * 2 * NY : (l + 1) * 2 * NY] for l in range(3)]
            plane = middle + jnp.where(z > 0, pltpu.roll(lower, 1, 1), 0.0)
            plane = plane + jnp.where(z < NZ - 1, pltpu.roll(upper, NZ - 1, 1), 0.0)
            planes_ref[at] = plane
            high, low = split(lower)
            cols = slice(at * 2 * NY, (at + 1) * 2 * NY)
            up_ref[:, cols] = dot_nt(pick_last, high) + dot_nt(pick_last, low)
            high, low = split(upper)
            down_ref[:, cols] = dot_nt(pick_first, high) + dot_nt(pick_first, low)


def conv_call(features, conv_weight, weight_step):
    return pl.pallas_call(
        conv_kernel,
        out_shape=(
            jax.ShapeDtypeStruct((6, 2 * NY, NZ), F32),
            jax.ShapeDtypeStruct((8, 6 * 2 * NY), F32),
            jax.ShapeDtypeStruct((8, 6 * 2 * NY), F32),
        ),
        in_specs=[pl.BlockSpec(memory_space=pltpu.VMEM)] * 3,
        out_specs=[pl.BlockSpec(memory_space=pltpu.VMEM)] * 3,
        scratch_shapes=[
            pltpu.VMEM((18 * NY, CY), BF16),
            pltpu.VMEM((CY, 6 * NZ), BF16),
        ],
        compiler_params=pltpu.CompilerParams(vmem_limit_bytes=VMEM_LIMIT),
    )(features, conv_weight, weight_step)


def place():
    gx, gy, gz = lax.axis_index("gx"), lax.axis_index("gy"), lax.axis_index("gz")
    slab = gx * 4 + gy
    right, left = lax.rem(slab + 1, 32), lax.rem(slab + 31, 32)
    sides = (
        (slab < 31, (right // 4, lax.rem(right, 4), gz)),
        (slab > 0, (left // 4, lax.rem(left, 4), gz)),
        (gz < 7, (gx, gy, lax.rem(gz + 1, 8))),
        (gz > 0, (gx, gy, lax.rem(gz + 7, 8))),
    )
    return slab, gz, sides


def propagate_kernel(
    planes_ref, up_ref, down_ref, bias_ref, wave_ref, born_ref, adj_ref, sx_ref, sy_ref, amp_ref,
    counts_ref, plane_t, halo_t, line_t, halo_z_t, pick_t,
    born_out, adj_out, shifted_out,
    waves, borns, drives, duals, parts, halves, from_x, edges, from_z,
    stiff, stiff_step, cot_scale, grad, spot, weight, conv_z, conv_x, rims, cot, cot_edge, cot_z,
    sx_sem, rx_sem, sz_sem, rz_sem, sc_sem, rc_sem,
):
    slab, gz, sides = place()
    (has_right, right), (has_left, left), (has_up, up), (has_down, down) = sides

    @pl.when(jnp.logical_not(has_left))
    def _():
        from_x[:, :, 0:ROWS, :] = jnp.zeros((2, 6, ROWS, NZ), BF16)
        conv_x[0] = jnp.zeros((2 * NY, NZ), F32)
        cot[0:NY] = jnp.zeros((NY, NZ), BF16)

    @pl.when(jnp.logical_not(has_right))
    def _():
        from_x[:, :, ROWS:, :] = jnp.zeros((2, 6, ROWS, NZ), BF16)
        conv_x[1] = jnp.zeros((2 * NY, NZ), F32)
        cot[5 * NY :] = jnp.zeros((NY, NZ), BF16)

    @pl.when(jnp.logical_not(has_down))
    def _():
        from_z[:, :, 0:16, :] = jnp.zeros((2, 6, 16, ROWS), BF16)
        conv_z[0] = jnp.zeros((8, 12 * NY), F32)
        cot_z[0] = jnp.zeros((16, 6 * NY), BF16)

    @pl.when(jnp.logical_not(has_up))
    def _():
        from_z[:, :, 16:, :] = jnp.zeros((2, 6, 16, ROWS), BF16)
        conv_z[1] = jnp.zeros((8, 12 * NY), F32)
        cot_z[1] = jnp.zeros((16, 6 * NY), BF16)

    barrier = pltpu.get_barrier_semaphore()
    for present, device in sides:
        @pl.when(present)
        def _(device=device):
            pl.semaphore_signal(barrier, inc=1, device_id=device, device_id_type=MESH)

    def remote(src, dst, send, recv, device):
        return pltpu.make_async_remote_copy(
            src_ref=src, dst_ref=dst, send_sem=send, recv_sem=recv,
            device_id=device, device_id_type=MESH,
        )

    def halo_copies(par, f):
        high = halves.at[par, f, pl.ds(0, ROWS)]
        return (
            (has_up, has_down, remote(
                edges.at[par, f, pl.ds(0, 16)], from_z.at[par, f, pl.ds(0, 16)],
                sz_sem.at[par, f, 0], rz_sem.at[par, f, 0], up)),
            (has_down, has_up, remote(
                edges.at[par, f, pl.ds(16, 16)], from_z.at[par, f, pl.ds(16, 16)],
                sz_sem.at[par, f, 1], rz_sem.at[par, f, 1], down)),
            (has_right, has_left, remote(
                high, from_x.at[par, f, pl.ds(0, ROWS)],
                sx_sem.at[par, f, 0], rx_sem.at[par, f, 0], right)),
            (has_left, has_right, remote(
                high, from_x.at[par, f, pl.ds(ROWS, ROWS)],
                sx_sem.at[par, f, 1], rx_sem.at[par, f, 1], left)),
        )

    def start(copies):
        for leaves, _, copy in copies:
            @pl.when(leaves)
            def _(copy=copy):
                copy.start()

    def wait_in(copies):
        for _, arrives, copy in copies:
            @pl.when(arrives)
            def _(copy=copy):
                copy.wait_recv()

    def wait_out(copies):
        for leaves, _, copy in copies:
            @pl.when(leaves)
            def _(copy=copy):
                copy.wait_send()

    def lay(par, f, values):
        high, low = split(values)
        halves[par, f, 0:ROWS] = high
        edges[par, f] = dot_nt(pick_t[...], high).astype(BF16)
        return high, low

    def inner(par, f, values, high, low):
        halves[par, f, ROWS:] = low
        part = dot(jnp.concatenate([high, low], axis=1), line_t[...])
        part = part + dot(plane_t[...], halves[par, f])
        parts[f] = part + CENTER5 * values

    def send(par, f, values):
        high, low = lay(par, f, values)
        start(halo_copies(par, f))
        inner(par, f, values, high, low)

    def laplace(par, f):
        wait_in(halo_copies(par, f))
        out = parts[f] + dot(halo_t[...], from_x[par, f])
        return 0.2 * (out + dot_tn(from_z[par, f], halo_z_t[...]))

    for s in range(2):
        waves[0, s] = wave_ref[0, s]
        waves[1, s] = wave_ref[1, s]
        borns[0, s] = born_ref[0, s]
        borns[1, s] = born_ref[1, s]
    firsts = [(f, (waves if f < 2 else borns)[1, f % 2]) for f in range(4)]
    rests = [(f, values, lay(0, f, values)) for f, values in firsts]

    pl.semaphore_wait(barrier, sum(jnp.where(present, 1, 0) for present, _ in sides))

    conv_z_copies = (
        (has_up, has_down, remote(up_ref, conv_z.at[0], sc_sem.at[0], rc_sem.at[0], up)),
        (has_down, has_up, remote(down_ref, conv_z.at[1], sc_sem.at[1], rc_sem.at[1], down)),
    )
    conv_x_copies = (
        (has_right, has_left, remote(
            rims.at[1], conv_x.at[0], sc_sem.at[2], rc_sem.at[2], right)),
        (has_left, has_right, remote(
            rims.at[0], conv_x.at[1], sc_sem.at[3], rc_sem.at[3], left)),
    )
    start(conv_z_copies)
    for f, _ in firsts:
        start(halo_copies(0, f))
    for f, values, (high, low) in rests:
        inner(0, f, values, high, low)

    row = iota((ROWS, NZ), 0)
    z = iota((ROWS, NZ), 1)
    top = jnp.where(gz == 0, 1.0, 0.0)
    for s in range(2):
        at = (sx_ref[s] - slab * SX) * NY + sy_ref[s]
        inside = (sx_ref[s] >= slab * SX) & (sx_ref[s] < slab * SX + SX)
        at = jnp.where(inside, at, -1)
        spot[s] = jnp.where((row == at) & (z == SRC_DEPTH), top, 0.0)
    weight[...] = jnp.where(z == REC_DEPTH, counts_ref[...] * counts_ref[...] * top, 0.0)

    wait_in(conv_z_copies)

    def rim_z(at):
        cols = slice(at * 2 * NY, (at + 1) * 2 * NY)
        total = planes_ref[at]
        for k, lane in ((0, 0), (1, NZ - 1)):
            pick = jnp.where((iota((8, NZ), 0) == 0) & (iota((8, NZ), 1) == lane), 1.0, 0.0)
            high, low = split(conv_z[k, :, cols])
            total = total + dot_tn(high, pick.astype(BF16)) + dot_tn(low, pick.astype(BF16))
        return total

    rims[0] = rim_z(0)
    rims[1] = rim_z(5)
    start(conv_x_copies)
    inner_planes = [rim_z(1), rim_z(2), rim_z(3), rim_z(4)]
    wait_in(conv_x_copies)
    inner_planes[0] = inner_planes[0] + conv_x[0]
    inner_planes[3] = inner_planes[3] + conv_x[1]
    for x in range(SX):
        rows = slice(x * NY, (x + 1) * NY)
        both = inner_planes[x]
        sigma = jax.nn.sigmoid(both[0:NY] + bias_ref[0])
        velocity = 1.5 + 3.0 * sigma
        slope = 3.0 * sigma * (1.0 - sigma)
        velocity_step = slope * both[NY:]
        stiff[rows] = QUOTIENT * velocity * velocity
        stiff_step[rows] = 2.0 * QUOTIENT * velocity * velocity_step
        cot_scale[rows] = slope * (2.0 * QUOTIENT * velocity)
    wait_out(conv_z_copies)
    wait_out(conv_x_copies)

    def advance(n, par, last):
        for s in range(2):
            drive = laplace(par, s)
            drives[n, s] = drive
            if not last:
                ahead = 2.0 * waves[n + 1, s] - waves[n, s] + stiff[...] * drive
                ahead = ahead + amp_ref[n] * spot[s]
                wait_out(halo_copies(par, s))
                send(1 - par, s, ahead)
                waves[n + 2, s] = ahead
            else:
                wait_out(halo_copies(par, s))
        for s in range(2):
            bent = laplace(par, 2 + s)
            ahead = 2.0 * borns[n + 1, s] - borns[n, s] + stiff[...] * bent
            ahead = ahead + stiff_step[...] * drives[n, s]
            wait_out(halo_copies(par, 2 + s))
            if not last:
                send(1 - par, 2 + s, ahead)
            borns[n + 2, s] = ahead

    def forward(n, carry):
        advance(n, lax.rem(n, 2), False)
        return carry

    lax.fori_loop(0, NT - 1, forward, 0)
    advance(NT - 1, (NT - 1) % 2, True)
    for s in range(2):
        born_out[0, s] = borns[NT, s]
        born_out[1, s] = borns[NT + 1, s]

    for s in range(2):
        newer = adj_ref[1, s] + weight[...] * borns[NT + 1, s]
        duals[0, s] = newer
        duals[1, s] = -adj_ref[0, s]
        send(0, 4 + s, stiff[...] * newer)
    grad[...] = jnp.zeros((ROWS, NZ), F32)

    def retreat(m, par, last):
        n = NT - 1 - m
        for s in range(2):
            newer = duals[0, s]
            grad[...] += newer * drives[n, s]
            base = 2.0 * newer - duals[1, s]
            if not last:
                base = base + weight[...] * borns[n + 1, s]
            current = base + laplace(par, 4 + s)
            wait_out(halo_copies(par, 4 + s))
            if not last:
                send(1 - par, 4 + s, stiff[...] * current)
            duals[1, s] = newer
            duals[0, s] = current

    def backward(m, carry):
        retreat(m, lax.rem(m, 2), False)
        return carry

    lax.fori_loop(0, NT - 1, backward, 0)
    retreat(NT - 1, (NT - 1) % 2, True)
    for s in range(2):
        adj_out[0, s] = -duals[1, s]
        adj_out[1, s] = duals[0, s]

    own = (cot_scale[...] * grad[...]).astype(BF16)
    cot[NY : 5 * NY] = own
    cot_x_copies = (
        (has_right, has_left, remote(
            cot.at[pl.ds(4 * NY, NY)], cot.at[pl.ds(0, NY)], sc_sem.at[4], rc_sem.at[4], right)),
        (has_left, has_right, remote(
            cot.at[pl.ds(NY, NY)], cot.at[pl.ds(5 * NY, NY)], sc_sem.at[5], rc_sem.at[5], left)),
    )
    start(cot_x_copies)
    wait_in(cot_x_copies)
    edge_lane = jnp.where(iota((32, NZ), 0) == 0, NZ - 1, jnp.where(iota((32, NZ), 0) == 16, 0, -1))
    edge_pick = jnp.where(iota((32, NZ), 1) == edge_lane, 1.0, 0.0).astype(BF16)
    wide = cot[...]
    cot_edge[...] = dot_nt(edge_pick, wide).astype(BF16)
    cot_z_copies = (
        (has_up, has_down, remote(
            cot_edge.at[pl.ds(0, 16)], cot_z.at[0], sc_sem.at[6], rc_sem.at[6], up)),
        (has_down, has_up, remote(
            cot_edge.at[pl.ds(16, 16)], cot_z.at[1], sc_sem.at[7], rc_sem.at[7], down)),
    )
    start(cot_z_copies)
    lanes = iota((6 * NY, NZ), 1)
    wide_f = wide.astype(F32)
    ahead = jnp.where(lanes < NZ - 1, pltpu.roll(wide_f, NZ - 1, 1), 0.0)
    behind = jnp.where(lanes > 0, pltpu.roll(wide_f, 1, 1), 0.0)
    wait_in(cot_z_copies)
    for k, values, lane in ((1, ahead, NZ - 1), (0, behind, 0)):
        pick = jnp.where((iota((16, NZ), 0) == 0) & (iota((16, NZ), 1) == lane), 1.0, 0.0)
        total = values + dot_tn(cot_z[k], pick.astype(BF16))
        shifted_out[2 * (1 - k)] = total.astype(BF16)
    shifted_out[1] = wide
    wait_out(cot_x_copies)
    wait_out(cot_z_copies)


def propagate_call(planes, rim_up, rim_down, bias, wave, born, adjoint, shot_x, shot_y, counts):
    steps = np.arange(NT, dtype=np.float64)
    spread = (0.45 * (steps - 5.0)) ** 2
    amplitude = (20.0 * (1.0 - 2.0 * spread) * np.exp(-spread)).astype(np.float32)
    vmem, smem = [pl.BlockSpec(memory_space=m) for m in (pltpu.VMEM, pltpu.SMEM)]
    pair = (2, ROWS, NZ)
    dma = pltpu.SemaphoreType.DMA
    return pl.pallas_call(
        propagate_kernel,
        out_shape=(
            jax.ShapeDtypeStruct((2, *pair), F32),
            jax.ShapeDtypeStruct((2, *pair), F32),
            jax.ShapeDtypeStruct((3, 6 * NY, NZ), BF16),
        ),
        in_specs=[vmem] * 3 + [smem] + [vmem] * 3 + [smem] * 3 + [vmem] * 6,
        out_specs=[vmem] * 3,
        scratch_shapes=[
            pltpu.VMEM((NT + 2, *pair), F32),
            pltpu.VMEM((NT + 2, *pair), F32),
            pltpu.VMEM((NT, *pair), F32),
            pltpu.VMEM((2, *pair), F32),
            pltpu.VMEM((6, ROWS, NZ), F32),
            pltpu.VMEM((2, 6, 2 * ROWS, NZ), BF16),
            pltpu.VMEM((2, 6, 2 * ROWS, NZ), BF16),
            pltpu.VMEM((2, 6, 32, ROWS), BF16),
            pltpu.VMEM((2, 6, 32, ROWS), BF16),
            pltpu.VMEM((ROWS, NZ), F32),
            pltpu.VMEM((ROWS, NZ), F32),
            pltpu.VMEM((ROWS, NZ), F32),
            pltpu.VMEM((ROWS, NZ), F32),
            pltpu.VMEM(pair, F32),
            pltpu.VMEM((ROWS, NZ), F32),
            pltpu.VMEM((2, 8, 12 * NY), F32),
            pltpu.VMEM((2, 2 * NY, NZ), F32),
            pltpu.VMEM((2, 2 * NY, NZ), F32),
            pltpu.VMEM((6 * NY, NZ), BF16),
            pltpu.VMEM((32, 6 * NY), BF16),
            pltpu.VMEM((2, 16, 6 * NY), BF16),
            dma((2, 6, 2)), dma((2, 6, 2)), dma((2, 6, 2)), dma((2, 6, 2)), dma((8,)), dma((8,)),
        ],
        compiler_params=pltpu.CompilerParams(
            collective_id=0, has_side_effects=True, vmem_limit_bytes=VMEM_LIMIT
        ),
    )(
        planes, rim_up, rim_down, bias, wave, born, adjoint, shot_x, shot_y,
        jnp.asarray(amplitude), counts, *[jnp.asarray(t) for t in stencil_tables()],
    )


def back_kernel(
    f_ref, s_ref, w_ref, fg_ref, out_ref,
    band, taps, moments, packed, from_z, from_x, from_y, sz_sem, rz_sem, sx_sem, rx_sem, sy_sem, ry_sem,
):
    gx, gy, gz = lax.axis_index("gx"), lax.axis_index("gy"), lax.axis_index("gz")
    groups = (
        (8, gz, lambda k: (gx, gy, k), from_z, sz_sem, rz_sem),
        (8, gx, lambda k: (k, gy, gz), from_x, sx_sem, rx_sem),
        (4, gy, lambda k: (gx, k, gz), from_y, sy_sem, ry_sem),
    )
    barrier = pltpu.get_barrier_semaphore()
    for size, me, device, *_ in groups:
        for step in range(1, size):
            pl.semaphore_signal(
                barrier, inc=1, device_id=device(lax.rem(me + step, size)), device_id_type=MESH
            )

    for x in range(SX):
        for i in range(3):
            for l in range(3):
                at = (i * 3 + l) * NY
                first = (x - i + 2) * NY
                taps[x // 2, at : at + NY, (x % 2) * NZ : (x % 2 + 1) * NZ] = (
                    s_ref[l, first : first + NY, :]
                )
    wide = 9 * NY
    lane = iota((27, wide), 1)
    tap = iota((27, wide), 0)
    il = lane // NY
    expanded = []
    for j in range(3):
        place_at = (il // 3 * 3 + j) * 3 + lax.rem(il, 3)
        expanded.append(dot(w_ref[...], jnp.where(tap == place_at, 1.0, 0.0).astype(BF16)))
    offset = iota((NY, wide), 0) - lax.rem(iota((NY, wide), 1), NY)
    for c in range(C):
        block = jnp.zeros((NY, wide), F32)
        for j in range(3):
            block = jnp.where(offset == j - 1, expanded[j][c : c + 1, :], block)
        band[c * NY : (c + 1) * NY, :] = block.astype(BF16)

    def moment_step(k, carry):
        start = pl.multiple_of(k * 8, 8)
        total = jnp.zeros((8 * NY, wide), F32)
        for pair in range(2):
            left = f_ref[pl.ds(start, 8), 2 * pair].reshape(8 * NY, NZ)
            right = f_ref[pl.ds(start, 8), 2 * pair + 1].reshape(8 * NY, NZ)
            total = total + dot_nt(jnp.concatenate([left, right], axis=1), taps[pair])
        total = total.reshape(8, NY, wide)
        for j in range(3):
            part = jnp.where((offset == j - 1)[None], total, 0.0)
            moments[j, pl.ds(start, 8), :] = jnp.sum(part, axis=1)
        return carry

    lax.fori_loop(0, C // 8, moment_step, 0)
    lane = iota((wide, NZ), 1)
    il = iota((wide, NZ), 0) // NY
    total = jnp.zeros((C, NZ), F32)
    for j in range(3):
        place_at = (il // 3 * 3 + j) * 3 + lax.rem(il, 3)
        pick = jnp.where(lane == place_at, 1.0, 0.0).astype(BF16)
        values = moments[j]
        for _ in range(3):
            high = values.astype(BF16)
            total = total + dot(high, pick)
            values = values - high.astype(F32)
    pack = total[0:8]
    for k in range(1, 4):
        pack = pack + pltpu.roll(total[8 * k : 8 * k + 8], 32 * k, 1)

    pl.semaphore_wait(barrier, sum(size - 1 for size, *_ in groups))

    def feature_step(k, carry):
        start = pl.multiple_of(k * 8, 8)
        rows = pl.ds(pl.multiple_of(k * 8 * NY, 8 * NY), 8 * NY)
        for pair in range(2):
            product = dot(band[rows, :], taps[pair]).astype(BF16)
            for half in range(2):
                fg_ref[pl.ds(start, 8), 2 * pair + half] = product[
                    :, half * NZ : (half + 1) * NZ
                ].reshape(8, NY, NZ)
        return carry

    for at, (size, me, device, slots, send_sem, recv_sem) in enumerate(groups):
        packed[at] = pack
        copies = []
        for step in range(1, size):
            copies.append(pltpu.make_async_remote_copy(
                src_ref=packed.at[at], dst_ref=slots.at[step], send_sem=send_sem.at[step],
                recv_sem=recv_sem.at[step], device_id=device(lax.rem(me + step, size)),
                device_id_type=MESH,
            ))
        for copy in copies:
            copy.start()
        if at == 0:
            lax.fori_loop(0, 2, feature_step, 0)
        elif at == 1:
            lax.fori_loop(2, 4, feature_step, 0)
        for copy in copies:
            copy.wait_recv()
        slots[0] = pack
        shares = [slots[step] for step in range(size)]
        pack = jnp.zeros((8, NZ), F32)
        for k in range(size):
            share = shares[0]
            for step in range(1, size):
                share = jnp.where(lax.rem(me - step + size, size) == k, shares[step], share)
            pack = pack + share
        for copy in copies:
            copy.wait_send()
    for k in range(4):
        out_ref[8 * k : 8 * k + 8, :] = pltpu.roll(pack, (NZ - 32 * k) % NZ, 1) if k else pack


def back_call(features, shifted, conv_weight):
    dma = pltpu.SemaphoreType.DMA
    return pl.pallas_call(
        back_kernel,
        out_shape=(
            jax.ShapeDtypeStruct((C, SX, NY, NZ), BF16),
            jax.ShapeDtypeStruct((C, NZ), F32),
        ),
        in_specs=[pl.BlockSpec(memory_space=pltpu.VMEM)] * 3,
        out_specs=[pl.BlockSpec(memory_space=pltpu.VMEM)] * 2,
        scratch_shapes=[
            pltpu.VMEM((CY, 9 * NY), BF16),
            pltpu.VMEM((2, 9 * NY, 2 * NZ), BF16),
            pltpu.VMEM((3, C, 9 * NY), F32),
            pltpu.VMEM((3, 8, NZ), F32),
            pltpu.VMEM((8, 8, NZ), F32),
            pltpu.VMEM((8, 8, NZ), F32),
            pltpu.VMEM((4, 8, NZ), F32),
            dma((8,)), dma((8,)), dma((8,)), dma((8,)), dma((4,)), dma((4,)),
        ],
        compiler_params=pltpu.CompilerParams(
            collective_id=1, has_side_effects=True, vmem_limit_bytes=VMEM_LIMIT
        ),
    )(features, shifted, conv_weight)


def shards(
    features, conv_weight, weight_step, conv_bias, wave_state, born_in, adjoint_in,
    shot_x, shot_y, rec_x, rec_y,
):
    slab = lax.axis_index(("gx", "gy"))
    rows = jnp.where(rec_x // SX == slab, lax.rem(rec_x, SX) * NY + rec_y, -1)
    hits = (rows[None, :] == jnp.arange(ROWS)[:, None]).astype(F32)
    counts = jnp.sum(hits, axis=1, keepdims=True)
    planes, rim_up, rim_down = conv_call(features, conv_weight, weight_step)
    flat = (2, 2, ROWS, NZ)
    born, adjoint, shifted = propagate_call(
        planes, rim_up, rim_down, conv_bias, wave_state.reshape(flat), born_in.reshape(flat),
        adjoint_in.reshape(flat), shot_x, shot_y, counts,
    )
    feature_grad, moment_sum = back_call(features, shifted, conv_weight)
    cells = ROWS * NZ * 256
    weight_product = moment_sum[:, :27] / math.sqrt(cells) + weight_step.astype(F32)
    shape = (2, 2, SX, NY, NZ)
    return born.reshape(shape), adjoint.reshape(shape), weight_product, feature_grad


def solution(mesh):
    grid = P(None, None, ("gx", "gy"), None, "gz")
    maps = P(None, ("gx", "gy"), None, "gz")
    return jax.shard_map(
        shards,
        mesh=mesh,
        in_specs=(maps, P(), P(), P(), grid, grid, grid, P(), P(), P(), P()),
        out_specs=(grid, grid, P(), maps),
        check_vma=False,
    )
```

```python
import math

import jax
import jax.numpy as jnp
import ml_dtypes
import numpy as np
from jax import lax
from jax.experimental import pallas as pl
from jax.experimental.pallas import tpu as pltpu
from jax.sharding import PartitionSpec as P

NT = 12
SRC_DEPTH = 6
REC_DEPTH = 2
QUOTIENT = 0.0074
COEFFS5 = (8.0, -1.0, 8.0 / 63.0, -1.0 / 112.0)
CENTER5 = 15.0 * (-205.0 / 72.0)

C = 32
SX = 4
NY = 64
NZ = 128
ROWS = SX * NY
CY = C * NY
MESH = pl.DeviceIdType.MESH
F32 = jnp.float32
BF16 = jnp.bfloat16
VMEM_LIMIT = 58 * 2**20


def coefficient(distance):
    out = np.zeros(distance.shape, np.float32)
    for reach in range(1, 5):
        out[distance == reach] = COEFFS5[reach - 1]
    return out


def stencil_tables():
    row = np.arange(ROWS)
    x, y = row // NY, row % NY
    dx, dy = x[:, None] - x[None, :], y[:, None] - y[None, :]
    same_x, same_y = (dx == 0), (dy == 0)
    plane = coefficient(np.abs(dx)) * same_y + coefficient(np.abs(dy)) * same_x
    plane = np.concatenate([plane, plane], axis=1)
    left = coefficient(dx + SX) * same_y
    right = coefficient(SX - dx) * same_y
    halo_x = np.concatenate([left, right], axis=1)
    z = np.arange(NZ)
    line = coefficient(np.abs(z[:, None] - z[None, :]))
    line = np.concatenate([line, line], axis=0)
    halo_z = np.zeros((32, NZ), np.float32)
    pick = np.zeros((32, NZ), np.float32)
    for k in range(4):
        halo_z[k] = coefficient(z + 4 - k)
        halo_z[16 + k] = coefficient(NZ + k - z)
        pick[k, NZ - 4 + k] = 1.0
        pick[16 + k, k] = 1.0
    return [t.astype(ml_dtypes.bfloat16) for t in (plane, halo_x, line, halo_z, pick)]


def dot(a, b):
    return jnp.dot(a, b, preferred_element_type=F32)


def dot_nt(a, b):
    return lax.dot_general(a, b, (((1,), (1,)), ((), ())), preferred_element_type=F32)


def dot_tn(a, b):
    return lax.dot_general(a, b, (((0,), (0,)), ((), ())), preferred_element_type=F32)


def split(values):
    high = values.astype(BF16)
    return high, (values - high.astype(F32)).astype(BF16)


def iota(shape, dim):
    return lax.broadcasted_iota(jnp.int32, shape, dim)


def place():
    gx, gy, gz = lax.axis_index("gx"), lax.axis_index("gy"), lax.axis_index("gz")
    slab = gx * 4 + gy

    def at(step_x, step_z):
        other = lax.rem(slab + 32 + step_x, 32)
        return (other // 4, lax.rem(other, 4), lax.rem(gz + 8 + step_z, 8))

    inside = {1: (slab < 31, gz < 7), -1: (slab > 0, gz > 0)}
    sides = {}
    for dx in (1, 0, -1):
        for dz in (0, 1, -1):
            if dx == 0 and dz == 0:
                continue
            present = None
            if dx:
                present = inside[dx][0]
            if dz:
                present = inside[dz][1] if present is None else present & inside[dz][1]
            sides[dx, dz] = (present, at(dx, dz))
    return slab, gz, sides


def column(rows, lane):
    picked = (iota((rows, NZ), 0) == 0) & (iota((rows, NZ), 1) == lane)
    return jnp.where(picked, 1.0, 0.0).astype(BF16)


def kernel(
    f_hbm, w_ref, v_ref, bias_ref, wave_hbm, born_hbm, adj_hbm, sx_ref, sy_ref, rx_ref, ry_ref,
    amp_ref, plane_t, halo_t, line_t, halo_z_t, pick_t,
    born_out, adj_out, fg_out, weight_out,
    feats, band, wide, planes, rim_z, conv_x, conv_z, conv_c,
    waves, borns, drives, adjoint, duals, parts, base, halves, from_x, edges, from_z,
    stiff, stiff5, stiff_step, cot_scale, grad, spot, weight,
    cot, cot_edge, cot_z, cot_c, taps, moments, packed, slots, grads,
    in_sem, out_sem, sx_sem, rx_sem, sz_sem, rz_sem, sc_sem, rc_sem, sr_sem, rr_sem,
):
    slab, gz, sides = place()
    gx, gy = lax.axis_index("gx"), lax.axis_index("gy")
    loads = [
        pltpu.make_async_copy(f_hbm, feats, in_sem.at[0]),
        pltpu.make_async_copy(wave_hbm, waves.at[pl.ds(0, 2)], in_sem.at[1]),
        pltpu.make_async_copy(born_hbm, borns.at[pl.ds(0, 2)], in_sem.at[2]),
        pltpu.make_async_copy(adj_hbm, adjoint, in_sem.at[3]),
    ]
    for load in loads:
        load.start()

    def clear(side, writes):
        @pl.when(jnp.logical_not(sides[side][0]))
        def _():
            for ref in writes:
                ref[...] = jnp.zeros(ref.shape, ref.dtype)

    clear((-1, 0), [from_x.at[:, :, pl.ds(0, ROWS)], conv_x.at[0], cot.at[pl.ds(0, NY)]])
    clear((1, 0), [from_x.at[:, :, pl.ds(ROWS, ROWS)], conv_x.at[1], cot.at[pl.ds(5 * NY, NY)]])
    clear((0, -1), [from_z.at[:, :, pl.ds(0, 16)], conv_z.at[0], cot_z.at[0]])
    clear((0, 1), [from_z.at[:, :, pl.ds(16, 16)], conv_z.at[1], cot_z.at[1]])
    for k, dz in enumerate((-1, 1)):
        for h, dx in enumerate((-1, 1)):
            clear((dx, dz), [conv_c.at[k, h], cot_c.at[k, h]])

    in_z = gz * 2 + lax.rem(gy, 2)
    in_x = gx * 2 + gy // 2
    groups = (
        (in_z, lambda k: (gx, gy // 2 * 2 + lax.rem(k, 2), k // 2)),
        (in_x, lambda k: (k // 2, lax.rem(k, 2) * 2 + lax.rem(gy, 2), gz)),
    )
    barrier = pltpu.get_barrier_semaphore()
    for present, device in sides.values():
        @pl.when(present)
        def _(device=device):
            pl.semaphore_signal(barrier, inc=1, device_id=device, device_id_type=MESH)
    for me, device in groups:
        for step in range(1, 16):
            pl.semaphore_signal(
                barrier, inc=1, device_id=device(lax.rem(me + step, 16)), device_id_type=MESH
            )

    def remote(src, dst, send, recv, device):
        return pltpu.make_async_remote_copy(
            src_ref=src, dst_ref=dst, send_sem=send, recv_sem=recv,
            device_id=device, device_id_type=MESH,
        )

    def start(exchange):
        for side, copy in exchange.items():
            @pl.when(sides[side][0])
            def _(copy=copy):
                copy.start()

    def finish(exchange):
        for dx, dz in exchange:
            @pl.when(sides[dx, dz][0])
            def _(dx=dx, dz=dz):
                exchange[-dx, -dz].wait_recv()
                exchange[dx, dz].wait_send()

    def x_halo(par, f):
        high = halves.at[par, f, pl.ds(0, ROWS)]
        return {
            (dx, 0): remote(
                high, from_x.at[par, f, pl.ds(k * ROWS, ROWS)],
                sx_sem.at[par, f, k], rx_sem.at[par, f, k], sides[dx, 0][1])
            for k, dx in enumerate((1, -1))
        }

    def z_halo(par, f):
        return {
            (0, dz): remote(
                edges.at[par, f, pl.ds(16 * k, 16)], from_z.at[par, f, pl.ds(16 * k, 16)],
                sz_sem.at[par, f, k], rz_sem.at[par, f, k], sides[0, dz][1])
            for k, dz in enumerate((1, -1))
        }

    def send(par, f, values):
        high, low = split(values)
        halves[par, f, 0:ROWS] = high
        start(x_halo(par, f))
        edges[par, f] = dot_nt(pick_t[...], high).astype(BF16)
        start(z_halo(par, f))
        return high, low

    def inner(par, f, values, high, low):
        halves[par, f, ROWS:] = low
        part = dot(jnp.concatenate([high, low], axis=1), line_t[...])
        part = part + dot(plane_t[...], halves[par, f])
        return part + CENTER5 * values

    def outer(par, f):
        finish({**z_halo(par, f), **x_halo(par, f)})
        return dot(halo_t[...], from_x[par, f]) + dot_tn(from_z[par, f], halo_z_t[...])

    repeat = jnp.where(iota((C, CY), 1) // NY == iota((C, CY), 0), 1.0, 0.0).astype(BF16)
    expanded = [dot_tn(w_ref[...], repeat), dot_tn(v_ref[...], repeat)]
    offset = lax.rem(iota((NY, CY), 1), NY) - iota((NY, CY), 0)
    for i in range(3):
        for l in range(3):
            for o in range(2):
                block = jnp.zeros((NY, CY), F32)
                for j in range(3):
                    tap = (i * 3 + j) * 3 + l
                    block = jnp.where(offset == j - 1, expanded[o][tap : tap + 1, :], block)
                first = ((i * 3 + l) * 2 + o) * NY
                band[first : first + NY, :] = block.astype(BF16)
    wide[:, 0:NZ] = jnp.zeros((CY, NZ), BF16)
    wide[:, 5 * NZ : 6 * NZ] = jnp.zeros((CY, NZ), BF16)
    loads[0].wait()
    for x in range(SX):
        wide[:, (x + 1) * NZ : (x + 2) * NZ] = feats[:, x].reshape(CY, NZ)
    lanes = iota((2 * NY, NZ), 1)

    def generate(pair):
        total = None
        for i in range(3):
            first = 2 * pair + i - 1
            if first < 0 or first > 4:
                continue
            term = dot(
                band[i * 6 * NY : (i + 1) * 6 * NY, :], wide[:, first * NZ : (first + 2) * NZ]
            )
            total = term if total is None else total + term
        for half in range(2):
            at = 2 * pair + half
            part = total[:, half * NZ : (half + 1) * NZ]
            lower, middle, upper = [part[l * 2 * NY : (l + 1) * 2 * NY] for l in range(3)]
            plane = middle + jnp.where(lanes > 0, pltpu.roll(lower, 1, 1), 0.0)
            planes[at] = plane + jnp.where(lanes < NZ - 1, pltpu.roll(upper, NZ - 1, 1), 0.0)
            for k, edge, lane in ((0, lower, NZ - 1), (1, upper, 0)):
                high, low = split(edge)
                rim_z[k, at] = dot_nt(column(8, lane), high) + dot_nt(column(8, lane), low)

    rims = {}
    for k, dx in enumerate((1, -1)):
        rims[dx, 0] = remote(
            planes.at[5 if dx > 0 else 0], conv_x.at[k], sc_sem.at[k], rc_sem.at[k],
            sides[dx, 0][1])
        for h, dz in enumerate((1, -1)):
            n = 4 + 2 * h + k
            rims[dx, dz] = remote(
                rim_z.at[h, 5 if dx > 0 else 0], conv_c.at[h, k], sc_sem.at[n], rc_sem.at[n],
                sides[dx, dz][1])
    depths = {
        (0, dz): remote(
            rim_z.at[h, pl.ds(1, 4)], conv_z.at[h], sc_sem.at[2 + h], rc_sem.at[2 + h],
            sides[0, dz][1])
        for h, dz in enumerate((1, -1))
    }

    generate(0)
    generate(2)
    pl.semaphore_wait(
        barrier, 30 + sum(jnp.where(present, 1, 0) for present, _ in sides.values())
    )
    start(rims)
    generate(1)
    start(depths)
    loads[1].wait()
    loads[2].wait()
    loads[3].wait()
    for f in range(4):
        values = (waves if f < 2 else borns)[1, f % 2]
        parts[f] = inner(0, f, values, *send(0, f, values))

    row = iota((ROWS, NZ), 0)
    z = iota((ROWS, NZ), 1)
    top = jnp.where(gz == 0, 1.0, 0.0)
    for s in range(2):
        at = (sx_ref[s] - slab * SX) * NY + sy_ref[s]
        inside = (sx_ref[s] >= slab * SX) & (sx_ref[s] < slab * SX + SX)
        at = jnp.where(inside, at, -1)
        spot[s] = jnp.where((row == at) & (z == SRC_DEPTH), top, 0.0)
    cells = jnp.where(
        rx_ref[...] // SX == slab, lax.rem(rx_ref[...], SX) * NY + ry_ref[...], -1
    )
    hits = jnp.zeros((ROWS, NZ), F32)
    for k in range(8):
        hits = hits + jnp.where(row == cells[k : k + 1, :], 1.0, 0.0)
    counts = jnp.sum(hits, axis=1, keepdims=True)
    weight[...] = jnp.where(z == REC_DEPTH, counts * counts * top, 0.0)

    def unpack(edge, lane):
        high, low = split(edge)
        return dot_tn(high, column(8, lane)) + dot_tn(low, column(8, lane))

    finish({**rims, **depths})
    for x in range(SX):
        rows = slice(x * NY, (x + 1) * NY)
        both = planes[x + 1]
        for h, lane in ((0, 0), (1, NZ - 1)):
            both = both + unpack(conv_z[h, x], lane)
            if x == 0:
                both = both + unpack(conv_c[h, 0], lane)
            if x == SX - 1:
                both = both + unpack(conv_c[h, 1], lane)
        if x == 0:
            both = both + conv_x[0]
        if x == SX - 1:
            both = both + conv_x[1]
        sigma = jax.nn.sigmoid(both[0:NY] + bias_ref[0])
        velocity = 1.5 + 3.0 * sigma
        slope = 3.0 * sigma * (1.0 - sigma)
        velocity_step = slope * both[NY:]
        stiffness = QUOTIENT * velocity * velocity
        stiff[rows] = stiffness
        stiff5[rows] = 0.2 * stiffness
        stiff_step[rows] = 2.0 * QUOTIENT * velocity * velocity_step
        cot_scale[rows] = slope * (2.0 * QUOTIENT * velocity)

    for s in range(2):
        base[s] = 2.0 * waves[1, s] - waves[0, s] + amp_ref[0] * spot[s] + stiff5[...] * parts[s]
        base[2 + s] = 2.0 * borns[1, s] - borns[0, s] + stiff5[...] * parts[2 + s]

    def advance(n, par, last):
        for s in range(2):
            rest = outer(par, s)
            if not last:
                ahead = base[s] + stiff5[...] * rest
                high, low = send(1 - par, s, ahead)
            drive = 0.2 * (parts[s] + rest)
            drives[n, s] = drive
            base[2 + s] += stiff_step[...] * drive
            if not last:
                part = inner(1 - par, s, ahead, high, low)
                parts[s] = part
                waves[n + 2, s] = ahead
                base[s] = (
                    2.0 * ahead - waves[n + 1, s] + amp_ref[n + 1] * spot[s] + stiff5[...] * part
                )
        for s in range(2):
            f = 2 + s
            ahead = base[f] + stiff5[...] * outer(par, f)
            if not last:
                high, low = send(1 - par, f, ahead)
                part = inner(1 - par, f, ahead, high, low)
                base[f] = 2.0 * ahead - borns[n + 1, s] + stiff5[...] * part
            borns[n + 2, s] = ahead

    def forward(n, carry):
        advance(n, lax.rem(n, 2), False)
        return carry

    lax.fori_loop(0, NT - 1, forward, 0)
    advance(NT - 1, (NT - 1) % 2, True)
    stores = [pltpu.make_async_copy(borns.at[pl.ds(NT, 2)], born_out, out_sem.at[0])]
    stores[0].start()

    def settle(n, s, newer, newest, part):
        duals[0, s] = newer
        duals[1, s] = newest
        base[4 + s] = 2.0 * newer - newest + weight[...] * borns[n, s] + 0.2 * part

    for s in range(2):
        newer = adjoint[1, s] + weight[...] * borns[NT + 1, s]
        bent = stiff[...] * newer
        part = inner(0, 4 + s, bent, *send(0, 4 + s, bent))
        settle(NT, s, newer, -adjoint[0, s], part)
    grad[...] = duals[0, 0] * drives[NT - 1, 0] + duals[0, 1] * drives[NT - 1, 1]

    def retreat(m, par):
        n = NT - 1 - m
        for s in range(2):
            current = base[4 + s] + 0.2 * outer(par, 4 + s)
            bent = stiff[...] * current
            part = inner(1 - par, 4 + s, bent, *send(1 - par, 4 + s, bent))
            grad[...] += current * drives[n - 1, s]
            settle(n, s, current, duals[0, s], part)

    def backward(m, carry):
        retreat(m, lax.rem(m, 2))
        return carry

    lax.fori_loop(0, NT - 1, backward, 0)

    cot[NY : 5 * NY] = (cot_scale[...] * grad[...]).astype(BF16)
    own = cot[NY : 5 * NY]
    edge_lane = jnp.where(iota((32, NZ), 0) == 0, NZ - 1, jnp.where(iota((32, NZ), 0) == 16, 0, -1))
    edge_pick = jnp.where(iota((32, NZ), 1) == edge_lane, 1.0, 0.0).astype(BF16)
    around = {}
    for k, dx in enumerate((1, -1)):
        around[dx, 0] = remote(
            cot.at[pl.ds(4 * NY if dx > 0 else NY, NY)],
            cot.at[pl.ds(0 if dx > 0 else 5 * NY, NY)],
            sc_sem.at[8 + k], rc_sem.at[8 + k], sides[dx, 0][1])
    for h, dz in enumerate((1, -1)):
        around[0, dz] = remote(
            cot_edge.at[pl.ds(16 * h, 16)], cot_z.at[h],
            sc_sem.at[10 + h], rc_sem.at[10 + h], sides[0, dz][1])
        for k, dx in enumerate((1, -1)):
            n = 12 + 2 * h + k
            around[dx, dz] = remote(
                cot_edge.at[pl.ds(16 * h, 16), pl.ds(2 * NY if dx > 0 else 0, 2 * NY)],
                cot_c.at[h, k], sc_sem.at[n], rc_sem.at[n], sides[dx, dz][1])
    cot_edge[...] = dot_nt(edge_pick, own).astype(BF16)
    start(around)

    for s in range(2):
        adjoint[0, s] = -duals[0, s]
        adjoint[1, s] = base[4 + s] - weight[...] * borns[1, s] + 0.2 * outer((NT - 1) % 2, 4 + s)
    stores.append(pltpu.make_async_copy(adjoint, adj_out, out_sem.at[1]))
    stores[1].start()

    span = 9 * NY
    il = iota((27, span), 1) // NY
    expanded = []
    for j in range(3):
        tap = (il // 3 * 3 + j) * 3 + lax.rem(il, 3)
        expanded.append(dot(w_ref[...], jnp.where(iota((27, span), 0) == tap, 1.0, 0.0).astype(BF16)))
    offset = iota((NY, span), 0) - lax.rem(iota((NY, span), 1), NY)
    for c in range(C):
        block = jnp.zeros((NY, span), F32)
        for j in range(3):
            block = jnp.where(offset == j - 1, expanded[j][c : c + 1, :], block)
        grads[c * NY : (c + 1) * NY, :] = block.astype(BF16)

    finish(around)
    lanes = iota((6 * NY, NZ), 1)
    whole = cot[...].astype(F32)
    shifted = {1: cot[...]}
    for l, h, lane, turn in ((0, 1, NZ - 1, NZ - 1), (2, 0, 0, 1)):
        inside = jnp.where(lanes == lane, 0.0, pltpu.roll(whole, turn, 1))
        pick = column(16, lane)
        rim = jnp.concatenate(
            [
                dot_tn(cot_c[h, 0], pick)[NY:],
                dot_tn(cot_z[h], pick),
                dot_tn(cot_c[h, 1], pick)[:NY],
            ],
            axis=0,
        )
        shifted[l] = (inside + rim).astype(BF16)
    for x in range(SX):
        for i in range(3):
            for l in range(3):
                at = (i * 3 + l) * NY
                first = (x - i + 2) * NY
                taps[x // 2, at : at + NY, (x % 2) * NZ : (x % 2 + 1) * NZ] = (
                    shifted[l][first : first + NY, :]
                )

    def moment_step(k, carry):
        first = pl.multiple_of(k * 8, 8)
        rows = pl.ds(pl.multiple_of(k * 8 * NY, 8 * NY), 8 * NY)
        total = dot_nt(wide[rows, NZ : 3 * NZ], taps[0]) + dot_nt(wide[rows, 3 * NZ : 5 * NZ], taps[1])
        total = total.reshape(8, NY, span)
        for j in range(3):
            part = jnp.where((offset == j - 1)[None], total, 0.0)
            moments[j, pl.ds(first, 8), :] = jnp.sum(part, axis=1)
        return carry

    lax.fori_loop(0, C // 8, moment_step, 0)
    il = iota((span, NZ), 0) // NY
    total = jnp.zeros((C, NZ), F32)
    for j in range(3):
        tap = (il // 3 * 3 + j) * 3 + lax.rem(il, 3)
        pick = jnp.where(iota((span, NZ), 1) == tap, 1.0, 0.0).astype(BF16)
        values = moments[j]
        for _ in range(3):
            high = values.astype(BF16)
            total = total + dot(high, pick)
            values = values - high.astype(F32)
    pack = total[0:8]
    for k in range(1, 4):
        pack = pack + pltpu.roll(total[8 * k : 8 * k + 8], 32 * k, 1)

    def feature_step(k, carry):
        first = pl.multiple_of(k * 8, 8)
        rows = pl.ds(pl.multiple_of(k * 8 * NY, 8 * NY), 8 * NY)
        for pair in range(2):
            product = dot(grads[rows, :], taps[pair]).astype(BF16)
            for half in range(2):
                feats[pl.ds(first, 8), 2 * pair + half] = product[
                    :, half * NZ : (half + 1) * NZ
                ].reshape(8, NY, NZ)
        return carry

    for g, (me, device) in enumerate(groups):
        packed[g] = pack
        slots[g, me] = pack
        copies = []
        for step in range(1, 16):
            copies.append(remote(
                packed.at[g], slots.at[g, me], sr_sem.at[g, step], rr_sem.at[g, me],
                device(lax.rem(me + step, 16)),
            ))
            copies[-1].start()
        lax.fori_loop(2 * g, 2 * g + 2, feature_step, 0)
        half = pl.ds(16 * g, 16)
        stores.append(pltpu.make_async_copy(feats.at[half], fg_out.at[half], out_sem.at[2 + g]))
        stores[-1].start()
        for step in range(1, 16):
            k = lax.rem(me + step, 16)
            remote(
                packed.at[g], slots.at[g, k], sr_sem.at[g, step], rr_sem.at[g, k], device(k)
            ).wait_recv()
        for copy in copies:
            copy.wait_send()
        pack = slots[g, 0]
        for k in range(1, 16):
            pack = pack + slots[g, k]
    scale = 1.0 / math.sqrt(ROWS * NZ * 256)
    for k in range(4):
        rows = slice(8 * k, 8 * k + 8)
        values = pltpu.roll(pack, NZ - 32 * k, 1) if k else pack
        weight_out[rows, :] = values[:, :27] * scale + v_ref[...][rows].astype(F32)
    for store in stores:
        store.wait()


def shards(
    features, conv_weight, weight_step, conv_bias, wave_state, born_in, adjoint_in,
    shot_x, shot_y, rec_x, rec_y,
):
    steps = np.arange(NT, dtype=np.float64)
    spread = (0.45 * (steps - 5.0)) ** 2
    amplitude = (20.0 * (1.0 - 2.0 * spread) * np.exp(-spread)).astype(np.float32)
    hbm, vmem, smem = [
        pl.BlockSpec(memory_space=m) for m in (pl.ANY, pltpu.VMEM, pltpu.SMEM)
    ]
    field = (ROWS, NZ)
    pair = (2, *field)
    dma = pltpu.SemaphoreType.DMA
    born, adjoint, feature_grad, weight_product = pl.pallas_call(
        kernel,
        out_shape=(
            jax.ShapeDtypeStruct((2, *pair), F32),
            jax.ShapeDtypeStruct((2, *pair), F32),
            jax.ShapeDtypeStruct((C, SX, NY, NZ), BF16),
            jax.ShapeDtypeStruct((C, 27), F32),
        ),
        in_specs=[hbm, vmem, vmem, smem, hbm, hbm, hbm, smem, smem, vmem, vmem, smem] + [vmem] * 5,
        out_specs=[hbm, hbm, hbm, vmem],
        scratch_shapes=[
            pltpu.VMEM((C, SX, NY, NZ), BF16),
            pltpu.VMEM((18 * NY, CY), BF16),
            pltpu.VMEM((CY, 6 * NZ), BF16),
            pltpu.VMEM((6, 2 * NY, NZ), F32),
            pltpu.VMEM((2, 6, 8, 2 * NY), F32),
            pltpu.VMEM((2, 2 * NY, NZ), F32),
            pltpu.VMEM((2, 4, 8, 2 * NY), F32),
            pltpu.VMEM((2, 2, 8, 2 * NY), F32),
            pltpu.VMEM((NT + 2, *pair), F32),
            pltpu.VMEM((NT + 2, *pair), F32),
            pltpu.VMEM((NT, *pair), F32),
            pltpu.VMEM((2, *pair), F32),
            pltpu.VMEM((2, *pair), F32),
            pltpu.VMEM((4, *field), F32),
            pltpu.VMEM((6, *field), F32),
            pltpu.VMEM((2, 6, 2 * ROWS, NZ), BF16),
            pltpu.VMEM((2, 6, 2 * ROWS, NZ), BF16),
            pltpu.VMEM((2, 6, 32, ROWS), BF16),
            pltpu.VMEM((2, 6, 32, ROWS), BF16),
            pltpu.VMEM(field, F32),
            pltpu.VMEM(field, F32),
            pltpu.VMEM(field, F32),
            pltpu.VMEM(field, F32),
            pltpu.VMEM(field, F32),
            pltpu.VMEM(pair, F32),
            pltpu.VMEM(field, F32),
            pltpu.VMEM((6 * NY, NZ), BF16),
            pltpu.VMEM((32, ROWS), BF16),
            pltpu.VMEM((2, 16, ROWS), BF16),
            pltpu.VMEM((2, 2, 16, 2 * NY), BF16),
            pltpu.VMEM((2, 9 * NY, 2 * NZ), BF16),
            pltpu.VMEM((3, C, 9 * NY), F32),
            pltpu.VMEM((2, 8, NZ), F32),
            pltpu.VMEM((2, 16, 8, NZ), F32),
            pltpu.VMEM((CY, 9 * NY), BF16),
            dma((4,)), dma((4,)),
            dma((2, 6, 2)), dma((2, 6, 2)), dma((2, 6, 2)), dma((2, 6, 2)),
            dma((16,)), dma((16,)), dma((2, 16)), dma((2, 16)),
        ],
        compiler_params=pltpu.CompilerParams(
            collective_id=0, has_side_effects=True, vmem_limit_bytes=VMEM_LIMIT
        ),
    )(
        features, conv_weight, weight_step, conv_bias,
        *[v.reshape(2, *pair) for v in (wave_state, born_in, adjoint_in)],
        shot_x, shot_y, rec_x.reshape(8, 128), rec_y.reshape(8, 128),
        jnp.asarray(amplitude), *[jnp.asarray(t) for t in stencil_tables()],
    )
    shape = (2, 2, SX, NY, NZ)
    return born.reshape(shape), adjoint.reshape(shape), weight_product, feature_grad


def solution(mesh):
    grid = P(None, None, ("gx", "gy"), None, "gz")
    maps = P(None, ("gx", "gy"), None, "gz")
    return jax.shard_map(
        shards,
        mesh=mesh,
        in_specs=(maps, P(), P(), P(), grid, grid, grid, P(), P(), P(), P()),
        out_specs=(grid, grid, P(), maps),
        check_vma=False,
    )
```

```python
import math

import jax
import jax.numpy as jnp
import ml_dtypes
import numpy as np
from jax import lax
from jax.experimental import pallas as pl
from jax.experimental.pallas import tpu as pltpu
from jax.sharding import PartitionSpec as P

NT = 12
SRC_DEPTH = 6
REC_DEPTH = 2
QUOTIENT = 0.0074
COEFFS5 = (8.0, -1.0, 8.0 / 63.0, -1.0 / 112.0)
CENTER5 = 15.0 * (-205.0 / 72.0)

C = 32
SX = 4
NY = 64
NZ = 128
ROWS = SX * NY
CY = C * NY
MESH = pl.DeviceIdType.MESH
F32 = jnp.float32
BF16 = jnp.bfloat16
VMEM_LIMIT = 58 * 2**20


def coefficient(distance):
    out = np.zeros(distance.shape, np.float32)
    for reach in range(1, 5):
        out[distance == reach] = COEFFS5[reach - 1]
    return out


def stencil_tables():
    row = np.arange(ROWS)
    x, y = row // NY, row % NY
    dx, dy = x[:, None] - x[None, :], y[:, None] - y[None, :]
    same_x, same_y = (dx == 0), (dy == 0)
    plane = coefficient(np.abs(dx)) * same_y + coefficient(np.abs(dy)) * same_x
    plane = np.concatenate([plane, plane], axis=1)
    z = np.arange(NZ)
    line = coefficient(np.abs(z[:, None] - z[None, :]))
    line = np.concatenate([line, line], axis=0)
    halo_z = np.zeros((32, NZ), np.float32)
    pick = np.zeros((32, NZ), np.float32)
    for k in range(4):
        halo_z[k] = coefficient(z + 4 - k)
        halo_z[16 + k] = coefficient(NZ + k - z)
        pick[k, NZ - 4 + k] = 1.0
        pick[16 + k, k] = 1.0
    return [t.astype(ml_dtypes.bfloat16) for t in (plane, line, halo_z, pick)]


def dot(a, b):
    return jnp.dot(a, b, preferred_element_type=F32)


def dot_nt(a, b):
    return lax.dot_general(a, b, (((1,), (1,)), ((), ())), preferred_element_type=F32)


def dot_tn(a, b):
    return lax.dot_general(a, b, (((0,), (0,)), ((), ())), preferred_element_type=F32)


def split(values):
    high = values.astype(BF16)
    return high, (values - high.astype(F32)).astype(BF16)


def iota(shape, dim):
    return lax.broadcasted_iota(jnp.int32, shape, dim)


def place():
    gx, gy, gz = lax.axis_index("gx"), lax.axis_index("gy"), lax.axis_index("gz")
    slab = gx * 4 + gy

    def at(step_x, step_z):
        other = lax.rem(slab + 32 + step_x, 32)
        return (other // 4, lax.rem(other, 4), lax.rem(gz + 8 + step_z, 8))

    inside = {1: (slab < 31, gz < 7), -1: (slab > 0, gz > 0)}
    sides = {}
    for dx in (1, 0, -1):
        for dz in (0, 1, -1):
            if dx == 0 and dz == 0:
                continue
            present = None
            if dx:
                present = inside[dx][0]
            if dz:
                present = inside[dz][1] if present is None else present & inside[dz][1]
            sides[dx, dz] = (present, at(dx, dz))
    return slab, gz, sides


def column(rows, lane):
    picked = (iota((rows, NZ), 0) == 0) & (iota((rows, NZ), 1) == lane)
    return jnp.where(picked, 1.0, 0.0).astype(BF16)


def kernel(
    f_hbm, w_ref, v_ref, bias_ref, wave_hbm, born_hbm, adj_hbm, sx_ref, sy_ref, rx_ref, ry_ref,
    amp_ref, plane_t, line_t, halo_z_t, pick_t,
    born_out, adj_out, fg_out, weight_out,
    feats, band, wide, planes, rim_z, conv_x, conv_z, conv_c,
    waves, borns, drives, adjoint, duals, parts, base, halves, from_x, edges, from_z,
    stiff, stiff5, stiff_step, cot_scale, grad, spot, weight,
    cot, cot_edge, cot_z, cot_c, taps, moments, packed, slots, grads,
    in_sem, out_sem, sx_sem, rx_sem, sz_sem, rz_sem, sc_sem, rc_sem, sr_sem, rr_sem,
):
    slab, gz, sides = place()
    gx, gy = lax.axis_index("gx"), lax.axis_index("gy")
    loads = [
        pltpu.make_async_copy(f_hbm, feats, in_sem.at[0]),
        pltpu.make_async_copy(wave_hbm, waves.at[pl.ds(0, 2)], in_sem.at[1]),
        pltpu.make_async_copy(born_hbm, borns.at[pl.ds(0, 2)], in_sem.at[2]),
        pltpu.make_async_copy(adj_hbm, adjoint, in_sem.at[3]),
    ]
    for load in loads:
        load.start()

    def clear(side, writes):
        @pl.when(jnp.logical_not(sides[side][0]))
        def _():
            for ref in writes:
                ref[...] = jnp.zeros(ref.shape, ref.dtype)

    clear((-1, 0), [from_x.at[:, :, pl.ds(0, ROWS)], conv_x.at[0], cot.at[pl.ds(0, NY)]])
    clear((1, 0), [from_x.at[:, :, pl.ds(ROWS, ROWS)], conv_x.at[1], cot.at[pl.ds(5 * NY, NY)]])
    clear((0, -1), [from_z.at[:, :, pl.ds(0, 16)], conv_z.at[0], cot_z.at[0]])
    clear((0, 1), [from_z.at[:, :, pl.ds(16, 16)], conv_z.at[1], cot_z.at[1]])
    for k, dz in enumerate((-1, 1)):
        for h, dx in enumerate((-1, 1)):
            clear((dx, dz), [conv_c.at[k, h], cot_c.at[k, h]])

    in_z = gz * 2 + lax.rem(gy, 2)
    in_x = gx * 2 + gy // 2
    groups = (
        (in_z, lambda k: (gx, gy // 2 * 2 + lax.rem(k, 2), k // 2)),
        (in_x, lambda k: (k // 2, lax.rem(k, 2) * 2 + lax.rem(gy, 2), gz)),
    )
    barrier = pltpu.get_barrier_semaphore()
    for present, device in sides.values():
        @pl.when(present)
        def _(device=device):
            pl.semaphore_signal(barrier, inc=1, device_id=device, device_id_type=MESH)
    for me, device in groups:
        for step in range(1, 16):
            pl.semaphore_signal(
                barrier, inc=1, device_id=device(lax.rem(me + step, 16)), device_id_type=MESH
            )

    def remote(src, dst, send, recv, device):
        return pltpu.make_async_remote_copy(
            src_ref=src, dst_ref=dst, send_sem=send, recv_sem=recv,
            device_id=device, device_id_type=MESH,
        )

    def start(exchange):
        for side, copy in exchange.items():
            @pl.when(sides[side][0])
            def _(copy=copy):
                copy.start()

    def finish(exchange):
        for dx, dz in exchange:
            @pl.when(sides[dx, dz][0])
            def _(dx=dx, dz=dz):
                exchange[-dx, -dz].wait_recv()
                exchange[dx, dz].wait_send()

    def x_halo(par, f):
        high = halves.at[par, f, pl.ds(0, ROWS)]
        return {
            (dx, 0): remote(
                high, from_x.at[par, f, pl.ds(k * ROWS, ROWS)],
                sx_sem.at[par, f, k], rx_sem.at[par, f, k], sides[dx, 0][1])
            for k, dx in enumerate((1, -1))
        }

    def z_halo(par, f):
        return {
            (0, dz): remote(
                edges.at[par, f, pl.ds(16 * k, 16)], from_z.at[par, f, pl.ds(16 * k, 16)],
                sz_sem.at[par, f, k], rz_sem.at[par, f, k], sides[0, dz][1])
            for k, dz in enumerate((1, -1))
        }

    def send(par, f, values):
        high, low = split(values)
        halves[par, f, 0:ROWS] = high
        start(x_halo(par, f))
        edges[par, f] = dot_nt(pick_t[...], high).astype(BF16)
        start(z_halo(par, f))
        return high, low

    def inner(par, f, values, high, low):
        halves[par, f, ROWS:] = low
        part = dot(jnp.concatenate([high, low], axis=1), line_t[...])
        part = part + dot(plane_t[...], halves[par, f])
        return part + CENTER5 * values

    def outer_z(par, f):
        finish(z_halo(par, f))
        return dot_tn(from_z[par, f], halo_z_t[...])

    def outer_x(par, f):
        finish(x_halo(par, f))
        left, right = [
            [from_x[par, f, pl.ds((k * SX + x) * NY, NY)].astype(F32) for x in range(SX)]
            for k in range(2)
        ]
        out = []
        for x in range(SX):
            total = None
            for reach in range(4, 0, -1):
                for there, have in ((x - reach + SX, left), (x + reach - SX, right)):
                    if 0 <= there < SX:
                        term = COEFFS5[reach - 1] * have[there]
                        total = term if total is None else total + term
            out.append(total)
        return jnp.concatenate(out, axis=0)

    repeat = jnp.where(iota((C, CY), 1) // NY == iota((C, CY), 0), 1.0, 0.0).astype(BF16)
    expanded = [dot_tn(w_ref[...], repeat), dot_tn(v_ref[...], repeat)]
    offset = lax.rem(iota((NY, CY), 1), NY) - iota((NY, CY), 0)
    for i in range(3):
        for l in range(3):
            for o in range(2):
                block = jnp.zeros((NY, CY), F32)
                for j in range(3):
                    tap = (i * 3 + j) * 3 + l
                    block = jnp.where(offset == j - 1, expanded[o][tap : tap + 1, :], block)
                first = ((i * 3 + l) * 2 + o) * NY
                band[first : first + NY, :] = block.astype(BF16)
    wide[:, 0:NZ] = jnp.zeros((CY, NZ), BF16)
    wide[:, 5 * NZ : 6 * NZ] = jnp.zeros((CY, NZ), BF16)
    loads[0].wait()
    for x in range(SX):
        wide[:, (x + 1) * NZ : (x + 2) * NZ] = feats[:, x].reshape(CY, NZ)
    lanes = iota((2 * NY, NZ), 1)

    def generate(pair):
        total = None
        for i in range(3):
            first = 2 * pair + i - 1
            if first < 0 or first > 4:
                continue
            term = dot(
                band[i * 6 * NY : (i + 1) * 6 * NY, :], wide[:, first * NZ : (first + 2) * NZ]
            )
            total = term if total is None else total + term
        for half in range(2):
            at = 2 * pair + half
            part = total[:, half * NZ : (half + 1) * NZ]
            lower, middle, upper = [part[l * 2 * NY : (l + 1) * 2 * NY] for l in range(3)]
            plane = middle + jnp.where(lanes > 0, pltpu.roll(lower, 1, 1), 0.0)
            planes[at] = plane + jnp.where(lanes < NZ - 1, pltpu.roll(upper, NZ - 1, 1), 0.0)
            for k, edge, lane in ((0, lower, NZ - 1), (1, upper, 0)):
                high, low = split(edge)
                rim_z[k, at] = dot_nt(column(8, lane), high) + dot_nt(column(8, lane), low)

    rims = {}
    for k, dx in enumerate((1, -1)):
        rims[dx, 0] = remote(
            planes.at[5 if dx > 0 else 0], conv_x.at[k], sc_sem.at[k], rc_sem.at[k],
            sides[dx, 0][1])
        for h, dz in enumerate((1, -1)):
            n = 4 + 2 * h + k
            rims[dx, dz] = remote(
                rim_z.at[h, 5 if dx > 0 else 0], conv_c.at[h, k], sc_sem.at[n], rc_sem.at[n],
                sides[dx, dz][1])
    depths = {
        (0, dz): remote(
            rim_z.at[h, pl.ds(1, 4)], conv_z.at[h], sc_sem.at[2 + h], rc_sem.at[2 + h],
            sides[0, dz][1])
        for h, dz in enumerate((1, -1))
    }

    generate(0)
    generate(2)
    pl.semaphore_wait(
        barrier, 30 + sum(jnp.where(present, 1, 0) for present, _ in sides.values())
    )
    start(rims)
    generate(1)
    start(depths)
    loads[1].wait()
    loads[2].wait()
    loads[3].wait()
    for f in range(4):
        values = (waves if f < 2 else borns)[1, f % 2]
        parts[f] = inner(0, f, values, *send(0, f, values))

    row = iota((ROWS, NZ), 0)
    z = iota((ROWS, NZ), 1)
    top = jnp.where(gz == 0, 1.0, 0.0)
    for s in range(2):
        at = (sx_ref[s] - slab * SX) * NY + sy_ref[s]
        inside = (sx_ref[s] >= slab * SX) & (sx_ref[s] < slab * SX + SX)
        at = jnp.where(inside, at, -1)
        spot[s] = jnp.where((row == at) & (z == SRC_DEPTH), top, 0.0)
    cells = jnp.where(
        rx_ref[...] // SX == slab, lax.rem(rx_ref[...], SX) * NY + ry_ref[...], -1
    )
    hits = jnp.zeros((ROWS, NZ), F32)
    for k in range(8):
        hits = hits + jnp.where(row == cells[k : k + 1, :], 1.0, 0.0)
    counts = jnp.sum(hits, axis=1, keepdims=True)
    weight[...] = jnp.where(z == REC_DEPTH, counts * counts * top, 0.0)

    def unpack(edge, lane):
        high, low = split(edge)
        return dot_tn(high, column(8, lane)) + dot_tn(low, column(8, lane))

    finish({**rims, **depths})
    for x in range(SX):
        rows = slice(x * NY, (x + 1) * NY)
        both = planes[x + 1]
        for h, lane in ((0, 0), (1, NZ - 1)):
            both = both + unpack(conv_z[h, x], lane)
            if x == 0:
                both = both + unpack(conv_c[h, 0], lane)
            if x == SX - 1:
                both = both + unpack(conv_c[h, 1], lane)
        if x == 0:
            both = both + conv_x[0]
        if x == SX - 1:
            both = both + conv_x[1]
        sigma = jax.nn.sigmoid(both[0:NY] + bias_ref[0])
        velocity = 1.5 + 3.0 * sigma
        slope = 3.0 * sigma * (1.0 - sigma)
        velocity_step = slope * both[NY:]
        stiffness = QUOTIENT * velocity * velocity
        stiff[rows] = stiffness
        stiff5[rows] = 0.2 * stiffness
        stiff_step[rows] = 2.0 * QUOTIENT * velocity * velocity_step
        cot_scale[rows] = slope * (2.0 * QUOTIENT * velocity)

    for s in range(2):
        base[s] = 2.0 * waves[1, s] - waves[0, s] + amp_ref[0] * spot[s] + stiff5[...] * parts[s]
        base[2 + s] = 2.0 * borns[1, s] - borns[0, s] + stiff5[...] * parts[2 + s]

    def advance(n, par, last):
        for s in range(2):
            depth = outer_z(par, s)
            parts[s] += depth
            base[s] += stiff5[...] * depth
            rest = outer_x(par, s)
            if not last:
                ahead = base[s] + stiff5[...] * rest
                high, low = send(1 - par, s, ahead)
            drive = 0.2 * (parts[s] + rest)
            drives[n, s] = drive
            base[2 + s] += stiff_step[...] * drive
            if not last:
                part = inner(1 - par, s, ahead, high, low)
                parts[s] = part
                waves[n + 2, s] = ahead
                base[s] = (
                    2.0 * ahead - waves[n + 1, s] + amp_ref[n + 1] * spot[s] + stiff5[...] * part
                )
        for s in range(2):
            f = 2 + s
            base[f] += stiff5[...] * outer_z(par, f)
            ahead = base[f] + stiff5[...] * outer_x(par, f)
            if not last:
                high, low = send(1 - par, f, ahead)
                part = inner(1 - par, f, ahead, high, low)
                base[f] = 2.0 * ahead - borns[n + 1, s] + stiff5[...] * part
            borns[n + 2, s] = ahead

    def forward(n, carry):
        advance(n, lax.rem(n, 2), False)
        return carry

    lax.fori_loop(0, NT - 1, forward, 0)
    advance(NT - 1, (NT - 1) % 2, True)
    stores = [pltpu.make_async_copy(borns.at[pl.ds(NT, 2)], born_out, out_sem.at[0])]
    stores[0].start()

    def settle(n, s, newer, newest, part):
        duals[0, s] = newer
        duals[1, s] = newest
        base[4 + s] = 2.0 * newer - newest + weight[...] * borns[n, s] + 0.2 * part

    for s in range(2):
        newer = adjoint[1, s] + weight[...] * borns[NT + 1, s]
        bent = stiff[...] * newer
        part = inner(0, 4 + s, bent, *send(0, 4 + s, bent))
        settle(NT, s, newer, -adjoint[0, s], part)
    grad[...] = duals[0, 0] * drives[NT - 1, 0] + duals[0, 1] * drives[NT - 1, 1]

    def retreat(m, par):
        n = NT - 1 - m
        for s in range(2):
            base[4 + s] += 0.2 * outer_z(par, 4 + s)
            current = base[4 + s] + 0.2 * outer_x(par, 4 + s)
            bent = stiff[...] * current
            part = inner(1 - par, 4 + s, bent, *send(1 - par, 4 + s, bent))
            grad[...] += current * drives[n - 1, s]
            settle(n, s, current, duals[0, s], part)

    def backward(m, carry):
        retreat(m, lax.rem(m, 2))
        return carry

    lax.fori_loop(0, NT - 1, backward, 0)

    cot[NY : 5 * NY] = (cot_scale[...] * grad[...]).astype(BF16)
    own = cot[NY : 5 * NY]
    edge_lane = jnp.where(iota((32, NZ), 0) == 0, NZ - 1, jnp.where(iota((32, NZ), 0) == 16, 0, -1))
    edge_pick = jnp.where(iota((32, NZ), 1) == edge_lane, 1.0, 0.0).astype(BF16)
    around = {}
    for k, dx in enumerate((1, -1)):
        around[dx, 0] = remote(
            cot.at[pl.ds(4 * NY if dx > 0 else NY, NY)],
            cot.at[pl.ds(0 if dx > 0 else 5 * NY, NY)],
            sc_sem.at[8 + k], rc_sem.at[8 + k], sides[dx, 0][1])
    for h, dz in enumerate((1, -1)):
        around[0, dz] = remote(
            cot_edge.at[pl.ds(16 * h, 16)], cot_z.at[h],
            sc_sem.at[10 + h], rc_sem.at[10 + h], sides[0, dz][1])
        for k, dx in enumerate((1, -1)):
            n = 12 + 2 * h + k
            around[dx, dz] = remote(
                cot_edge.at[pl.ds(16 * h, 16), pl.ds(2 * NY if dx > 0 else 0, 2 * NY)],
                cot_c.at[h, k], sc_sem.at[n], rc_sem.at[n], sides[dx, dz][1])
    cot_edge[...] = dot_nt(edge_pick, own).astype(BF16)
    start(around)

    for s in range(2):
        adjoint[0, s] = -duals[0, s]
        f, par = 4 + s, (NT - 1) % 2
        base[f] += 0.2 * outer_z(par, f) - weight[...] * borns[1, s]
        adjoint[1, s] = base[f] + 0.2 * outer_x(par, f)
    stores.append(pltpu.make_async_copy(adjoint, adj_out, out_sem.at[1]))
    stores[1].start()

    span = 9 * NY
    il = iota((27, span), 1) // NY
    expanded = []
    for j in range(3):
        tap = (il // 3 * 3 + j) * 3 + lax.rem(il, 3)
        expanded.append(dot(w_ref[...], jnp.where(iota((27, span), 0) == tap, 1.0, 0.0).astype(BF16)))
    offset = iota((NY, span), 0) - lax.rem(iota((NY, span), 1), NY)
    for c in range(C):
        block = jnp.zeros((NY, span), F32)
        for j in range(3):
            block = jnp.where(offset == j - 1, expanded[j][c : c + 1, :], block)
        grads[c * NY : (c + 1) * NY, :] = block.astype(BF16)

    finish(around)
    lanes = iota((6 * NY, NZ), 1)
    whole = cot[...].astype(F32)
    shifted = {1: cot[...]}
    for l, h, lane, turn in ((0, 1, NZ - 1, NZ - 1), (2, 0, 0, 1)):
        inside = jnp.where(lanes == lane, 0.0, pltpu.roll(whole, turn, 1))
        pick = column(16, lane)
        rim = jnp.concatenate(
            [
                dot_tn(cot_c[h, 0], pick)[NY:],
                dot_tn(cot_z[h], pick),
                dot_tn(cot_c[h, 1], pick)[:NY],
            ],
            axis=0,
        )
        shifted[l] = (inside + rim).astype(BF16)
    for x in range(SX):
        for i in range(3):
            for l in range(3):
                at = (i * 3 + l) * NY
                first = (x - i + 2) * NY
                taps[x // 2, at : at + NY, (x % 2) * NZ : (x % 2 + 1) * NZ] = (
                    shifted[l][first : first + NY, :]
                )

    def moment_step(k, carry):
        first = pl.multiple_of(k * 8, 8)
        rows = pl.ds(pl.multiple_of(k * 8 * NY, 8 * NY), 8 * NY)
        total = dot_nt(wide[rows, NZ : 3 * NZ], taps[0]) + dot_nt(wide[rows, 3 * NZ : 5 * NZ], taps[1])
        total = total.reshape(8, NY, span)
        for j in range(3):
            part = jnp.where((offset == j - 1)[None], total, 0.0)
            moments[j, pl.ds(first, 8), :] = jnp.sum(part, axis=1)
        return carry

    lax.fori_loop(0, C // 8, moment_step, 0)
    il = iota((span, NZ), 0) // NY
    total = jnp.zeros((C, NZ), F32)
    for j in range(3):
        tap = (il // 3 * 3 + j) * 3 + lax.rem(il, 3)
        pick = jnp.where(iota((span, NZ), 1) == tap, 1.0, 0.0).astype(BF16)
        values = moments[j]
        for _ in range(3):
            high = values.astype(BF16)
            total = total + dot(high, pick)
            values = values - high.astype(F32)
    pack = total[0:8]
    for k in range(1, 4):
        pack = pack + pltpu.roll(total[8 * k : 8 * k + 8], 32 * k, 1)

    def feature_step(k, carry):
        first = pl.multiple_of(k * 8, 8)
        rows = pl.ds(pl.multiple_of(k * 8 * NY, 8 * NY), 8 * NY)
        for pair in range(2):
            product = dot(grads[rows, :], taps[pair]).astype(BF16)
            for half in range(2):
                feats[pl.ds(first, 8), 2 * pair + half] = product[
                    :, half * NZ : (half + 1) * NZ
                ].reshape(8, NY, NZ)
        return carry

    for g, (me, device) in enumerate(groups):
        packed[g] = pack
        slots[g, me] = pack
        copies = []
        for step in range(1, 16):
            copies.append(remote(
                packed.at[g], slots.at[g, me], sr_sem.at[g, step], rr_sem.at[g, me],
                device(lax.rem(me + step, 16)),
            ))
            copies[-1].start()
        lax.fori_loop(2 * g, 2 * g + 2, feature_step, 0)
        half = pl.ds(16 * g, 16)
        stores.append(pltpu.make_async_copy(feats.at[half], fg_out.at[half], out_sem.at[2 + g]))
        stores[-1].start()
        for step in range(1, 16):
            k = lax.rem(me + step, 16)
            remote(
                packed.at[g], slots.at[g, k], sr_sem.at[g, step], rr_sem.at[g, k], device(k)
            ).wait_recv()
        for copy in copies:
            copy.wait_send()
        pack = slots[g, 0]
        for k in range(1, 16):
            pack = pack + slots[g, k]
    scale = 1.0 / math.sqrt(ROWS * NZ * 256)
    for k in range(4):
        rows = slice(8 * k, 8 * k + 8)
        values = pltpu.roll(pack, NZ - 32 * k, 1) if k else pack
        weight_out[rows, :] = values[:, :27] * scale + v_ref[...][rows].astype(F32)
    for store in stores:
        store.wait()


def settle_kernel(*refs):
    ins, outs, bufs, sem_in, sem_out = refs[:4], refs[4:8], refs[8:12], refs[12], refs[13]
    loads, stores = [], []
    for n in range(4):
        loads.append(pltpu.make_async_copy(ins[n], bufs[n], sem_in.at[n]))
        stores.append(pltpu.make_async_copy(bufs[n], outs[n], sem_out.at[n]))
        loads[n].start()
    for n in (3, 0, 1, 2):
        loads[n].wait()
        stores[n].start()
    for store in stores:
        store.wait()


def settle_call(*arrays):
    dma = pltpu.SemaphoreType.DMA
    return pl.pallas_call(
        settle_kernel,
        out_shape=[jax.ShapeDtypeStruct(a.shape, a.dtype) for a in arrays],
        in_specs=[pl.BlockSpec(memory_space=pl.ANY)] * 4,
        out_specs=[pl.BlockSpec(memory_space=pl.ANY)] * 4,
        scratch_shapes=[pltpu.VMEM(a.shape, a.dtype) for a in arrays] + [dma((4,)), dma((4,))],
        compiler_params=pltpu.CompilerParams(vmem_limit_bytes=VMEM_LIMIT),
    )(*arrays)


def shards(
    features, conv_weight, weight_step, conv_bias, wave_state, born_in, adjoint_in,
    shot_x, shot_y, rec_x, rec_y,
):
    steps = np.arange(NT, dtype=np.float64)
    spread = (0.45 * (steps - 5.0)) ** 2
    amplitude = (20.0 * (1.0 - 2.0 * spread) * np.exp(-spread)).astype(np.float32)
    hbm, vmem, smem = [
        pl.BlockSpec(memory_space=m) for m in (pl.ANY, pltpu.VMEM, pltpu.SMEM)
    ]
    field = (ROWS, NZ)
    pair = (2, *field)
    dma = pltpu.SemaphoreType.DMA
    born, adjoint, feature_grad, weight_product = pl.pallas_call(
        kernel,
        out_shape=(
            jax.ShapeDtypeStruct((2, *pair), F32),
            jax.ShapeDtypeStruct((2, *pair), F32),
            jax.ShapeDtypeStruct((C, SX, NY, NZ), BF16),
            jax.ShapeDtypeStruct((C, 27), F32),
        ),
        in_specs=[hbm, vmem, vmem, smem, hbm, hbm, hbm, smem, smem, vmem, vmem, smem] + [vmem] * 4,
        out_specs=[hbm, hbm, hbm, vmem],
        scratch_shapes=[
            pltpu.VMEM((C, SX, NY, NZ), BF16),
            pltpu.VMEM((18 * NY, CY), BF16),
            pltpu.VMEM((CY, 6 * NZ), BF16),
            pltpu.VMEM((6, 2 * NY, NZ), F32),
            pltpu.VMEM((2, 6, 8, 2 * NY), F32),
            pltpu.VMEM((2, 2 * NY, NZ), F32),
            pltpu.VMEM((2, 4, 8, 2 * NY), F32),
            pltpu.VMEM((2, 2, 8, 2 * NY), F32),
            pltpu.VMEM((NT + 2, *pair), F32),
            pltpu.VMEM((NT + 2, *pair), F32),
            pltpu.VMEM((NT, *pair), F32),
            pltpu.VMEM((2, *pair), F32),
            pltpu.VMEM((2, *pair), F32),
            pltpu.VMEM((4, *field), F32),
            pltpu.VMEM((6, *field), F32),
            pltpu.VMEM((2, 6, 2 * ROWS, NZ), BF16),
            pltpu.VMEM((2, 6, 2 * ROWS, NZ), BF16),
            pltpu.VMEM((2, 6, 32, ROWS), BF16),
            pltpu.VMEM((2, 6, 32, ROWS), BF16),
            pltpu.VMEM(field, F32),
            pltpu.VMEM(field, F32),
            pltpu.VMEM(field, F32),
            pltpu.VMEM(field, F32),
            pltpu.VMEM(field, F32),
            pltpu.VMEM(pair, F32),
            pltpu.VMEM(field, F32),
            pltpu.VMEM((6 * NY, NZ), BF16),
            pltpu.VMEM((32, ROWS), BF16),
            pltpu.VMEM((2, 16, ROWS), BF16),
            pltpu.VMEM((2, 2, 16, 2 * NY), BF16),
            pltpu.VMEM((2, 9 * NY, 2 * NZ), BF16),
            pltpu.VMEM((3, C, 9 * NY), F32),
            pltpu.VMEM((2, 8, NZ), F32),
            pltpu.VMEM((2, 16, 8, NZ), F32),
            pltpu.VMEM((CY, 9 * NY), BF16),
            dma((4,)), dma((4,)),
            dma((2, 6, 2)), dma((2, 6, 2)), dma((2, 6, 2)), dma((2, 6, 2)),
            dma((16,)), dma((16,)), dma((2, 16)), dma((2, 16)),
        ],
        compiler_params=pltpu.CompilerParams(
            collective_id=0, has_side_effects=True, vmem_limit_bytes=VMEM_LIMIT
        ),
    )(
        features, conv_weight, weight_step, conv_bias,
        *[v.reshape(2, *pair) for v in (wave_state, born_in, adjoint_in)],
        shot_x, shot_y, rec_x.reshape(8, 128), rec_y.reshape(8, 128),
        jnp.asarray(amplitude), *[jnp.asarray(t) for t in stencil_tables()],
    )
    born, adjoint, feature_grad, weight_product = settle_call(
        born, adjoint, feature_grad, weight_product
    )
    shape = (2, 2, SX, NY, NZ)
    return born.reshape(shape), adjoint.reshape(shape), weight_product, feature_grad


def solution(mesh):
    grid = P(None, None, ("gx", "gy"), None, "gz")
    maps = P(None, ("gx", "gy"), None, "gz")
    return jax.shard_map(
        shards,
        mesh=mesh,
        in_specs=(maps, P(), P(), P(), grid, grid, grid, P(), P(), P(), P()),
        out_specs=(grid, grid, P(), maps),
        check_vma=False,
    )
```

```python
import math

import jax
import jax.numpy as jnp
import ml_dtypes
import numpy as np
from jax import lax
from jax.experimental import pallas as pl
from jax.experimental.pallas import tpu as pltpu
from jax.sharding import PartitionSpec as P

NT = 12
SRC_DEPTH = 6
REC_DEPTH = 2
QUOTIENT = 0.0074
COEFFS5 = (8.0, -1.0, 8.0 / 63.0, -1.0 / 112.0)
CENTER5 = 15.0 * (-205.0 / 72.0)

C = 32
SX = 4
NY = 64
NZ = 128
ROWS = SX * NY
PART = NY // 2
CY = C * NY
MESH = pl.DeviceIdType.MESH
F32 = jnp.float32
BF16 = jnp.bfloat16
VMEM_LIMIT = 58 * 2**20


def coefficient(distance):
    out = np.zeros(distance.shape, np.float32)
    for reach in range(1, 5):
        out[distance == reach] = COEFFS5[reach - 1]
    return out


def stencil_tables():
    row = np.arange(ROWS)
    x, y = row // NY, row % NY
    dx, dy = x[:, None] - x[None, :], y[:, None] - y[None, :]
    same_x, same_y = (dx == 0), (dy == 0)
    plane = coefficient(np.abs(dx)) * same_y + coefficient(np.abs(dy)) * same_x
    plane = np.concatenate([plane, plane], axis=1)
    z = np.arange(NZ)
    line = coefficient(np.abs(z[:, None] - z[None, :]))
    line = np.concatenate([line, line], axis=0)
    halo_z = np.zeros((32, NZ), np.float32)
    pick = np.zeros((32, NZ), np.float32)
    for k in range(4):
        halo_z[k] = coefficient(z + 4 - k)
        halo_z[16 + k] = coefficient(NZ + k - z)
        pick[k, NZ - 4 + k] = 1.0
        pick[16 + k, k] = 1.0
    return [t.astype(ml_dtypes.bfloat16) for t in (plane, line, halo_z, pick)]


def dot(a, b):
    return jnp.dot(a, b, preferred_element_type=F32)


def dot_nt(a, b):
    return lax.dot_general(a, b, (((1,), (1,)), ((), ())), preferred_element_type=F32)


def dot_tn(a, b):
    return lax.dot_general(a, b, (((0,), (0,)), ((), ())), preferred_element_type=F32)


def split(values):
    high = values.astype(BF16)
    return high, (values - high.astype(F32)).astype(BF16)


def iota(shape, dim):
    return lax.broadcasted_iota(jnp.int32, shape, dim)


def place():
    gx, gy, gz = lax.axis_index("gx"), lax.axis_index("gy"), lax.axis_index("gz")
    slab = gx * 4 + gy

    def at(step_x, step_z):
        other = lax.rem(slab + 32 + step_x, 32)
        return (other // 4, lax.rem(other, 4), lax.rem(gz + 8 + step_z, 8))

    inside = {1: (slab < 31, gz < 7), -1: (slab > 0, gz > 0)}
    sides = {}
    for dx in (1, 0, -1):
        for dz in (0, 1, -1):
            if dx == 0 and dz == 0:
                continue
            present = None
            if dx:
                present = inside[dx][0]
            if dz:
                present = inside[dz][1] if present is None else present & inside[dz][1]
            sides[dx, dz] = (present, at(dx, dz))
    return slab, gz, sides


def column(rows, lane):
    picked = (iota((rows, NZ), 0) == 0) & (iota((rows, NZ), 1) == lane)
    return jnp.where(picked, 1.0, 0.0).astype(BF16)


def kernel(
    f_hbm, w_ref, v_ref, bias_ref, wave_hbm, born_hbm, adj_hbm, sx_ref, sy_ref, rx_ref, ry_ref,
    amp_ref, plane_t, line_t, halo_z_t, pick_t,
    born_out, adj_out, fg_out, weight_out,
    feats, band, wide, planes, rim_z, conv_x, conv_z, conv_c,
    waves, borns, drives, adjoint, duals, parts, base, halves, from_x, edges, from_z,
    stiff, stiff5, stiff_step, cot_scale, grad, spot, weight,
    cot, cot_edge, cot_z, cot_c, taps, moments, packed, slots, grads,
    in_sem, out_sem, sx_sem, rx_sem, sz_sem, rz_sem, sc_sem, rc_sem, sr_sem, rr_sem,
):
    slab, gz, sides = place()
    gx, gy = lax.axis_index("gx"), lax.axis_index("gy")
    loads = [
        pltpu.make_async_copy(f_hbm, feats, in_sem.at[0]),
        pltpu.make_async_copy(wave_hbm, waves.at[pl.ds(0, 2)], in_sem.at[1]),
        pltpu.make_async_copy(born_hbm, borns.at[pl.ds(0, 2)], in_sem.at[2]),
        pltpu.make_async_copy(adj_hbm, adjoint, in_sem.at[3]),
    ]
    for load in loads:
        load.start()

    def clear(side, writes):
        @pl.when(jnp.logical_not(sides[side][0]))
        def _():
            for ref in writes:
                ref[...] = jnp.zeros(ref.shape, ref.dtype)

    clear((-1, 0), [from_x.at[:, :, :, 0], conv_x.at[0], cot.at[pl.ds(0, NY)]])
    clear((1, 0), [from_x.at[:, :, :, 1], conv_x.at[1], cot.at[pl.ds(5 * NY, NY)]])
    clear((0, -1), [from_z.at[:, :, pl.ds(0, 16)], conv_z.at[0], cot_z.at[0]])
    clear((0, 1), [from_z.at[:, :, pl.ds(16, 16)], conv_z.at[1], cot_z.at[1]])
    for k, dz in enumerate((-1, 1)):
        for h, dx in enumerate((-1, 1)):
            clear((dx, dz), [conv_c.at[k, h], cot_c.at[k, h]])

    in_z = gz * 2 + lax.rem(gy, 2)
    in_x = gx * 2 + gy // 2
    groups = (
        (in_z, lambda k: (gx, gy // 2 * 2 + lax.rem(k, 2), k // 2)),
        (in_x, lambda k: (k // 2, lax.rem(k, 2) * 2 + lax.rem(gy, 2), gz)),
    )
    barrier = pltpu.get_barrier_semaphore()
    for present, device in sides.values():
        @pl.when(present)
        def _(device=device):
            pl.semaphore_signal(barrier, inc=1, device_id=device, device_id_type=MESH)
    for me, device in groups:
        for step in range(1, 16):
            pl.semaphore_signal(
                barrier, inc=1, device_id=device(lax.rem(me + step, 16)), device_id_type=MESH
            )

    def remote(src, dst, send, recv, device):
        return pltpu.make_async_remote_copy(
            src_ref=src, dst_ref=dst, send_sem=send, recv_sem=recv,
            device_id=device, device_id_type=MESH,
        )

    def start(exchange):
        for side, copy in exchange.items():
            @pl.when(sides[side][0])
            def _(copy=copy):
                copy.start()

    def finish(exchange):
        for dx, dz in exchange:
            @pl.when(sides[dx, dz][0])
            def _(dx=dx, dz=dz):
                exchange[-dx, -dz].wait_recv()
                exchange[dx, dz].wait_send()

    def x_halo(par, f, h):
        high = halves.at[par, f, 0, :, pl.ds(h * PART, PART)]
        return {
            (dx, 0): remote(
                high, from_x.at[par, f, h, k],
                sx_sem.at[par, f, 2 * h + k], rx_sem.at[par, f, 2 * h + k], sides[dx, 0][1])
            for k, dx in enumerate((1, -1))
        }

    def z_halo(par, f):
        return {
            (0, dz): remote(
                edges.at[par, f, pl.ds(16 * k, 16)], from_z.at[par, f, pl.ds(16 * k, 16)],
                sz_sem.at[par, f, k], rz_sem.at[par, f, k], sides[0, dz][1])
            for k, dz in enumerate((1, -1))
        }

    def take(ref, at, h):
        return jnp.concatenate(
            [ref[(*at, pl.ds(x * NY + h * PART, PART))] for x in range(SX)], axis=0
        )

    def put(ref, at, h, values):
        for x in range(SX):
            ref[(*at, pl.ds(x * NY + h * PART, PART))] = values[x * PART : (x + 1) * PART]

    def send_x(par, f, h, values):
        halves[par, f, 0, :, pl.ds(h * PART, PART)] = values.astype(BF16).reshape(SX, PART, NZ)
        start(x_halo(par, f, h))

    def send_z(par, f):
        high = halves[par, f, 0].reshape(ROWS, NZ)
        edges[par, f] = dot_nt(pick_t[...], high).astype(BF16)
        start(z_halo(par, f))

    def inner(par, f, values):
        high = halves[par, f, 0].reshape(ROWS, NZ)
        low = (values - high.astype(F32)).astype(BF16)
        halves[par, f, 1] = low.reshape(SX, NY, NZ)
        part = dot(jnp.concatenate([high, low], axis=1), line_t[...])
        part = part + dot(plane_t[...], halves[par, f].reshape(2 * ROWS, NZ))
        return part + CENTER5 * values

    def outer_z(par, f):
        finish(z_halo(par, f))
        return dot_tn(from_z[par, f], halo_z_t[...])

    def outer_x(par, f, h):
        finish(x_halo(par, f, h))
        left, right = [
            [from_x[par, f, h, k, x].astype(F32) for x in range(SX)] for k in range(2)
        ]
        out = []
        for x in range(SX):
            total = None
            for reach in range(4, 0, -1):
                for there, have in ((x - reach + SX, left), (x + reach - SX, right)):
                    if 0 <= there < SX:
                        term = COEFFS5[reach - 1] * have[there]
                        total = term if total is None else total + term
            out.append(total)
        return jnp.concatenate(out, axis=0)

    repeat = jnp.where(iota((C, CY), 1) // NY == iota((C, CY), 0), 1.0, 0.0).astype(BF16)
    expanded = [dot_tn(w_ref[...], repeat), dot_tn(v_ref[...], repeat)]
    offset = lax.rem(iota((NY, NZ), 1), NY) - iota((NY, NZ), 0)
    hit = [offset == j - 1 for j in range(3)]
    for i in range(3):
        for l in range(3):
            for o in range(2):
                first = ((i * 3 + l) * 2 + o) * NY
                for at in range(0, CY, NZ):
                    block = jnp.zeros((NY, NZ), F32)
                    for j in range(3):
                        tap = (i * 3 + j) * 3 + l
                        block = jnp.where(hit[j], expanded[o][tap : tap + 1, at : at + NZ], block)
                    band[first : first + NY, at : at + NZ] = block.astype(BF16)
    wide[:, 0:NZ] = jnp.zeros((CY, NZ), BF16)
    wide[:, 5 * NZ : 6 * NZ] = jnp.zeros((CY, NZ), BF16)
    loads[0].wait()
    for x in range(SX):
        wide[:, (x + 1) * NZ : (x + 2) * NZ] = feats[:, x].reshape(CY, NZ)
    lanes = iota((2 * NY, NZ), 1)

    def generate(pair):
        total = None
        for i in range(3):
            first = 2 * pair + i - 1
            if first < 0 or first > 4:
                continue
            term = dot(
                band[i * 6 * NY : (i + 1) * 6 * NY, :], wide[:, first * NZ : (first + 2) * NZ]
            )
            total = term if total is None else total + term
        for half in range(2):
            at = 2 * pair + half
            part = total[:, half * NZ : (half + 1) * NZ]
            lower, middle, upper = [part[l * 2 * NY : (l + 1) * 2 * NY] for l in range(3)]
            plane = middle + jnp.where(lanes > 0, pltpu.roll(lower, 1, 1), 0.0)
            planes[at] = plane + jnp.where(lanes < NZ - 1, pltpu.roll(upper, NZ - 1, 1), 0.0)
            for k, edge, lane in ((0, lower, NZ - 1), (1, upper, 0)):
                high, low = split(edge)
                rim_z[k, at] = dot_nt(column(8, lane), high) + dot_nt(column(8, lane), low)

    rims = {}
    for k, dx in enumerate((1, -1)):
        rims[dx, 0] = remote(
            planes.at[5 if dx > 0 else 0], conv_x.at[k], sc_sem.at[k], rc_sem.at[k],
            sides[dx, 0][1])
        for h, dz in enumerate((1, -1)):
            n = 4 + 2 * h + k
            rims[dx, dz] = remote(
                rim_z.at[h, 5 if dx > 0 else 0], conv_c.at[h, k], sc_sem.at[n], rc_sem.at[n],
                sides[dx, dz][1])
    depths = {
        (0, dz): remote(
            rim_z.at[h, pl.ds(1, 4)], conv_z.at[h], sc_sem.at[2 + h], rc_sem.at[2 + h],
            sides[0, dz][1])
        for h, dz in enumerate((1, -1))
    }

    generate(0)
    generate(2)
    pl.semaphore_wait(
        barrier, 30 + sum(jnp.where(present, 1, 0) for present, _ in sides.values())
    )
    start(rims)
    generate(1)
    start(depths)
    loads[1].wait()
    loads[2].wait()
    loads[3].wait()
    for f in range(4):
        values = (waves if f < 2 else borns)[1, f % 2]
        for h in range(2):
            send_x(0, f, h, take(waves if f < 2 else borns, (1, f % 2), h))
        send_z(0, f)
        parts[f] = inner(0, f, values)

    row = iota((ROWS, NZ), 0)
    z = iota((ROWS, NZ), 1)
    top = jnp.where(gz == 0, 1.0, 0.0)
    for s in range(2):
        at = (sx_ref[s] - slab * SX) * NY + sy_ref[s]
        inside = (sx_ref[s] >= slab * SX) & (sx_ref[s] < slab * SX + SX)
        at = jnp.where(inside, at, -1)
        spot[s] = jnp.where((row == at) & (z == SRC_DEPTH), top, 0.0)
    cells = jnp.where(
        rx_ref[...] // SX == slab, lax.rem(rx_ref[...], SX) * NY + ry_ref[...], -1
    )
    hits = jnp.zeros((ROWS, NZ), F32)
    for k in range(8):
        hits = hits + jnp.where(row == cells[k : k + 1, :], 1.0, 0.0)
    counts = jnp.sum(hits, axis=1, keepdims=True)
    weight[...] = jnp.where(z == REC_DEPTH, counts * counts * top, 0.0)

    def unpack(edge, lane):
        high, low = split(edge)
        return dot_tn(high, column(8, lane)) + dot_tn(low, column(8, lane))

    finish({**rims, **depths})
    for x in range(SX):
        rows = slice(x * NY, (x + 1) * NY)
        both = planes[x + 1]
        for h, lane in ((0, 0), (1, NZ - 1)):
            both = both + unpack(conv_z[h, x], lane)
            if x == 0:
                both = both + unpack(conv_c[h, 0], lane)
            if x == SX - 1:
                both = both + unpack(conv_c[h, 1], lane)
        if x == 0:
            both = both + conv_x[0]
        if x == SX - 1:
            both = both + conv_x[1]
        sigma = jax.nn.sigmoid(both[0:NY] + bias_ref[0])
        velocity = 1.5 + 3.0 * sigma
        slope = 3.0 * sigma * (1.0 - sigma)
        velocity_step = slope * both[NY:]
        stiffness = QUOTIENT * velocity * velocity
        stiff[rows] = stiffness
        stiff5[rows] = 0.2 * stiffness
        stiff_step[rows] = 2.0 * QUOTIENT * velocity * velocity_step
        cot_scale[rows] = slope * (2.0 * QUOTIENT * velocity)

    for s in range(2):
        base[s] = 2.0 * waves[1, s] - waves[0, s] + amp_ref[0] * spot[s] + stiff5[...] * parts[s]
        base[2 + s] = 2.0 * borns[1, s] - borns[0, s] + stiff5[...] * parts[2 + s]

    def advance(n, par, last):
        for s in range(2):
            depth = outer_z(par, s)
            parts[s] += depth
            base[s] += stiff5[...] * depth
            rests = []
            for h in range(2):
                rests.append(outer_x(par, s, h))
                if not last:
                    ahead = take(base, (s,), h) + take(stiff5, (), h) * rests[h]
                    send_x(1 - par, s, h, ahead)
                    put(waves, (n + 2, s), h, ahead)
            if not last:
                send_z(1 - par, s)
            for h in range(2):
                drive = 0.2 * (take(parts, (s,), h) + rests[h])
                put(drives, (n, s), h, drive)
                more = take(base, (2 + s,), h) + take(stiff_step, (), h) * drive
                put(base, (2 + s,), h, more)
            if not last:
                ahead = waves[n + 2, s]
                part = inner(1 - par, s, ahead)
                parts[s] = part
                base[s] = (
                    2.0 * ahead - waves[n + 1, s] + amp_ref[n + 1] * spot[s] + stiff5[...] * part
                )
        for s in range(2):
            f = 2 + s
            base[f] += stiff5[...] * outer_z(par, f)
            for h in range(2):
                ahead = take(base, (f,), h) + take(stiff5, (), h) * outer_x(par, f, h)
                if not last:
                    send_x(1 - par, f, h, ahead)
                put(borns, (n + 2, s), h, ahead)
            if not last:
                send_z(1 - par, f)
                ahead = borns[n + 2, s]
                part = inner(1 - par, f, ahead)
                base[f] = 2.0 * ahead - borns[n + 1, s] + stiff5[...] * part

    def forward(n, carry):
        advance(n, lax.rem(n, 2), False)
        return carry

    lax.fori_loop(0, NT - 1, forward, 0)
    advance(NT - 1, (NT - 1) % 2, True)
    stores = [pltpu.make_async_copy(borns.at[pl.ds(NT, 2)], born_out, out_sem.at[0])]
    stores[0].start()

    def settle(n, s, newer, newest, part):
        duals[0, s] = newer
        duals[1, s] = newest
        base[4 + s] = 2.0 * newer - newest + weight[...] * borns[n, s] + 0.2 * part

    for s in range(2):
        newer = adjoint[1, s] + weight[...] * borns[NT + 1, s]
        parts[s] = newer
        for h in range(2):
            send_x(0, 4 + s, h, take(stiff, (), h) * take(parts, (s,), h))
        send_z(0, 4 + s)
        part = inner(0, 4 + s, stiff[...] * newer)
        settle(NT, s, newer, -adjoint[0, s], part)
    grad[...] = duals[0, 0] * drives[NT - 1, 0] + duals[0, 1] * drives[NT - 1, 1]

    def retreat(m, par):
        n = NT - 1 - m
        for s in range(2):
            f = 4 + s
            base[f] += 0.2 * outer_z(par, f)
            for h in range(2):
                current = take(base, (f,), h) + 0.2 * outer_x(par, f, h)
                send_x(1 - par, f, h, take(stiff, (), h) * current)
                put(parts, (s,), h, current)
            send_z(1 - par, f)
            current = parts[s]
            part = inner(1 - par, f, stiff[...] * current)
            grad[...] += current * drives[n - 1, s]
            settle(n, s, current, duals[0, s], part)

    def backward(m, carry):
        retreat(m, lax.rem(m, 2))
        return carry

    lax.fori_loop(0, NT - 1, backward, 0)

    cot[NY : 5 * NY] = (cot_scale[...] * grad[...]).astype(BF16)
    own = cot[NY : 5 * NY]
    edge_lane = jnp.where(iota((32, NZ), 0) == 0, NZ - 1, jnp.where(iota((32, NZ), 0) == 16, 0, -1))
    edge_pick = jnp.where(iota((32, NZ), 1) == edge_lane, 1.0, 0.0).astype(BF16)
    around = {}
    for k, dx in enumerate((1, -1)):
        around[dx, 0] = remote(
            cot.at[pl.ds(4 * NY if dx > 0 else NY, NY)],
            cot.at[pl.ds(0 if dx > 0 else 5 * NY, NY)],
            sc_sem.at[8 + k], rc_sem.at[8 + k], sides[dx, 0][1])
    for h, dz in enumerate((1, -1)):
        around[0, dz] = remote(
            cot_edge.at[pl.ds(16 * h, 16)], cot_z.at[h],
            sc_sem.at[10 + h], rc_sem.at[10 + h], sides[0, dz][1])
        for k, dx in enumerate((1, -1)):
            n = 12 + 2 * h + k
            around[dx, dz] = remote(
                cot_edge.at[pl.ds(16 * h, 16), pl.ds(2 * NY if dx > 0 else 0, 2 * NY)],
                cot_c.at[h, k], sc_sem.at[n], rc_sem.at[n], sides[dx, dz][1])
    cot_edge[...] = dot_nt(edge_pick, own).astype(BF16)
    start(around)

    span = 9 * NY
    il = iota((27, span), 1) // NY
    expanded = []
    for j in range(3):
        tap = (il // 3 * 3 + j) * 3 + lax.rem(il, 3)
        expanded.append(dot(w_ref[...], jnp.where(iota((27, span), 0) == tap, 1.0, 0.0).astype(BF16)))
    offset = iota((NY, span), 0) - lax.rem(iota((NY, span), 1), NY)
    for c in range(C):
        block = jnp.zeros((NY, span), F32)
        for j in range(3):
            block = jnp.where(offset == j - 1, expanded[j][c : c + 1, :], block)
        grads[c * NY : (c + 1) * NY, :] = block.astype(BF16)

    finish(around)
    lanes = iota((6 * NY, NZ), 1)
    whole = cot[...].astype(F32)
    shifted = {1: cot[...]}
    for l, h, lane, turn in ((0, 1, NZ - 1, NZ - 1), (2, 0, 0, 1)):
        inside = jnp.where(lanes == lane, 0.0, pltpu.roll(whole, turn, 1))
        pick = column(16, lane)
        rim = jnp.concatenate(
            [
                dot_tn(cot_c[h, 0], pick)[NY:],
                dot_tn(cot_z[h], pick),
                dot_tn(cot_c[h, 1], pick)[:NY],
            ],
            axis=0,
        )
        shifted[l] = (inside + rim).astype(BF16)
    for x in range(SX):
        for i in range(3):
            for l in range(3):
                at = (i * 3 + l) * NY
                first = (x - i + 2) * NY
                taps[x // 2, at : at + NY, (x % 2) * NZ : (x % 2 + 1) * NZ] = (
                    shifted[l][first : first + NY, :]
                )

    def moment_step(k, carry):
        first = pl.multiple_of(k * 8, 8)
        rows = pl.ds(pl.multiple_of(k * 8 * NY, 8 * NY), 8 * NY)
        total = dot_nt(wide[rows, NZ : 3 * NZ], taps[0]) + dot_nt(wide[rows, 3 * NZ : 5 * NZ], taps[1])
        total = total.reshape(8, NY, span)
        for j in range(3):
            part = jnp.where((offset == j - 1)[None], total, 0.0)
            moments[j, pl.ds(first, 8), :] = jnp.sum(part, axis=1)
        return carry

    lax.fori_loop(0, C // 8, moment_step, 0)
    il = iota((span, NZ), 0) // NY
    total = jnp.zeros((C, NZ), F32)
    for j in range(3):
        tap = (il // 3 * 3 + j) * 3 + lax.rem(il, 3)
        pick = jnp.where(iota((span, NZ), 1) == tap, 1.0, 0.0).astype(BF16)
        values = moments[j]
        for _ in range(3):
            high = values.astype(BF16)
            total = total + dot(high, pick)
            values = values - high.astype(F32)
    pack = total[0:8]
    for k in range(1, 4):
        pack = pack + pltpu.roll(total[8 * k : 8 * k + 8], 32 * k, 1)

    def feature_step(k, carry):
        first = pl.multiple_of(k * 8, 8)
        rows = pl.ds(pl.multiple_of(k * 8 * NY, 8 * NY), 8 * NY)
        for pair in range(2):
            product = dot(grads[rows, :], taps[pair]).astype(BF16)
            for half in range(2):
                feats[pl.ds(first, 8), 2 * pair + half] = product[
                    :, half * NZ : (half + 1) * NZ
                ].reshape(8, NY, NZ)
        return carry

    def finish_adjoint():
        for s in range(2):
            adjoint[0, s] = -duals[0, s]
            f, par = 4 + s, (NT - 1) % 2
            base[f] += 0.2 * outer_z(par, f) - weight[...] * borns[1, s]
            for h in range(2):
                put(adjoint, (1, s), h, take(base, (f,), h) + 0.2 * outer_x(par, f, h))
        stores.append(pltpu.make_async_copy(adjoint, adj_out, out_sem.at[1]))
        stores[-1].start()

    for g, (me, device) in enumerate(groups):
        packed[g] = pack
        slots[g, me] = pack
        copies = []
        for step in range(1, 16):
            copies.append(remote(
                packed.at[g], slots.at[g, me], sr_sem.at[g, step], rr_sem.at[g, me],
                device(lax.rem(me + step, 16)),
            ))
            copies[-1].start()
        if g == 0:
            finish_adjoint()
        lax.fori_loop(2 * g, 2 * g + 2, feature_step, 0)
        half = pl.ds(16 * g, 16)
        stores.append(pltpu.make_async_copy(feats.at[half], fg_out.at[half], out_sem.at[2 + g]))
        stores[-1].start()
        for step in range(1, 16):
            k = lax.rem(me + step, 16)
            remote(
                packed.at[g], slots.at[g, k], sr_sem.at[g, step], rr_sem.at[g, k], device(k)
            ).wait_recv()
        for copy in copies:
            copy.wait_send()
        pack = slots[g, 0]
        for k in range(1, 16):
            pack = pack + slots[g, k]
    scale = 1.0 / math.sqrt(ROWS * NZ * 256)
    for k in range(4):
        rows = slice(8 * k, 8 * k + 8)
        values = pltpu.roll(pack, NZ - 32 * k, 1) if k else pack
        weight_out[rows, :] = values[:, :27] * scale + v_ref[...][rows].astype(F32)
    for store in stores:
        store.wait()


def settle_kernel(*refs):
    ins, outs, bufs, sem_in, sem_out = refs[:4], refs[4:8], refs[8:12], refs[12], refs[13]
    loads, stores = [], []
    for n in range(4):
        loads.append(pltpu.make_async_copy(ins[n], bufs[n], sem_in.at[n]))
        stores.append(pltpu.make_async_copy(bufs[n], outs[n], sem_out.at[n]))
        loads[n].start()
    for n in (3, 0, 1, 2):
        loads[n].wait()
        stores[n].start()
    for store in stores:
        store.wait()


def settle_call(*arrays):
    dma = pltpu.SemaphoreType.DMA
    return pl.pallas_call(
        settle_kernel,
        out_shape=[jax.ShapeDtypeStruct(a.shape, a.dtype) for a in arrays],
        in_specs=[pl.BlockSpec(memory_space=pl.ANY)] * 4,
        out_specs=[pl.BlockSpec(memory_space=pl.ANY)] * 4,
        scratch_shapes=[pltpu.VMEM(a.shape, a.dtype) for a in arrays] + [dma((4,)), dma((4,))],
        compiler_params=pltpu.CompilerParams(vmem_limit_bytes=VMEM_LIMIT),
    )(*arrays)


def shards(
    features, conv_weight, weight_step, conv_bias, wave_state, born_in, adjoint_in,
    shot_x, shot_y, rec_x, rec_y,
):
    steps = np.arange(NT, dtype=np.float64)
    spread = (0.45 * (steps - 5.0)) ** 2
    amplitude = (20.0 * (1.0 - 2.0 * spread) * np.exp(-spread)).astype(np.float32)
    hbm, vmem, smem = [
        pl.BlockSpec(memory_space=m) for m in (pl.ANY, pltpu.VMEM, pltpu.SMEM)
    ]
    field = (ROWS, NZ)
    pair = (2, *field)
    dma = pltpu.SemaphoreType.DMA
    born, adjoint, feature_grad, weight_product = pl.pallas_call(
        kernel,
        out_shape=(
            jax.ShapeDtypeStruct((2, *pair), F32),
            jax.ShapeDtypeStruct((2, *pair), F32),
            jax.ShapeDtypeStruct((C, SX, NY, NZ), BF16),
            jax.ShapeDtypeStruct((C, 27), F32),
        ),
        in_specs=[hbm, vmem, vmem, smem, hbm, hbm, hbm, smem, smem, vmem, vmem, smem] + [vmem] * 4,
        out_specs=[hbm, hbm, hbm, vmem],
        scratch_shapes=[
            pltpu.VMEM((C, SX, NY, NZ), BF16),
            pltpu.VMEM((18 * NY, CY), BF16),
            pltpu.VMEM((CY, 6 * NZ), BF16),
            pltpu.VMEM((6, 2 * NY, NZ), F32),
            pltpu.VMEM((2, 6, 8, 2 * NY), F32),
            pltpu.VMEM((2, 2 * NY, NZ), F32),
            pltpu.VMEM((2, 4, 8, 2 * NY), F32),
            pltpu.VMEM((2, 2, 8, 2 * NY), F32),
            pltpu.VMEM((NT + 2, *pair), F32),
            pltpu.VMEM((NT + 2, *pair), F32),
            pltpu.VMEM((NT, *pair), F32),
            pltpu.VMEM((2, *pair), F32),
            pltpu.VMEM((2, *pair), F32),
            pltpu.VMEM((4, *field), F32),
            pltpu.VMEM((6, *field), F32),
            pltpu.VMEM((2, 6, 2, SX, NY, NZ), BF16),
            pltpu.VMEM((2, 6, 2, 2, SX, PART, NZ), BF16),
            pltpu.VMEM((2, 6, 32, ROWS), BF16),
            pltpu.VMEM((2, 6, 32, ROWS), BF16),
            pltpu.VMEM(field, F32),
            pltpu.VMEM(field, F32),
            pltpu.VMEM(field, F32),
            pltpu.VMEM(field, F32),
            pltpu.VMEM(field, F32),
            pltpu.VMEM(pair, F32),
            pltpu.VMEM(field, F32),
            pltpu.VMEM((6 * NY, NZ), BF16),
            pltpu.VMEM((32, ROWS), BF16),
            pltpu.VMEM((2, 16, ROWS), BF16),
            pltpu.VMEM((2, 2, 16, 2 * NY), BF16),
            pltpu.VMEM((2, 9 * NY, 2 * NZ), BF16),
            pltpu.VMEM((3, C, 9 * NY), F32),
            pltpu.VMEM((2, 8, NZ), F32),
            pltpu.VMEM((2, 16, 8, NZ), F32),
            pltpu.VMEM((CY, 9 * NY), BF16),
            dma((4,)), dma((4,)),
            dma((2, 6, 4)), dma((2, 6, 4)), dma((2, 6, 2)), dma((2, 6, 2)),
            dma((16,)), dma((16,)), dma((2, 16)), dma((2, 16)),
        ],
        compiler_params=pltpu.CompilerParams(
            collective_id=0, has_side_effects=True, vmem_limit_bytes=VMEM_LIMIT
        ),
    )(
        features, conv_weight, weight_step, conv_bias,
        *[v.reshape(2, *pair) for v in (wave_state, born_in, adjoint_in)],
        shot_x, shot_y, rec_x.reshape(8, 128), rec_y.reshape(8, 128),
        jnp.asarray(amplitude), *[jnp.asarray(t) for t in stencil_tables()],
    )
    born, adjoint, feature_grad, weight_product = settle_call(
        born, adjoint, feature_grad, weight_product
    )
    shape = (2, 2, SX, NY, NZ)
    return born.reshape(shape), adjoint.reshape(shape), weight_product, feature_grad


def solution(mesh):
    grid = P(None, None, ("gx", "gy"), None, "gz")
    maps = P(None, ("gx", "gy"), None, "gz")
    return jax.shard_map(
        shards,
        mesh=mesh,
        in_specs=(maps, P(), P(), P(), grid, grid, grid, P(), P(), P(), P()),
        out_specs=(grid, grid, P(), maps),
        check_vma=False,
    )
```

```python
import math

import jax
import jax.numpy as jnp
import ml_dtypes
import numpy as np
from jax import lax
from jax.experimental import pallas as pl
from jax.experimental.pallas import tpu as pltpu
from jax.sharding import PartitionSpec as P

NT = 12
SRC_DEPTH = 6
REC_DEPTH = 2
QUOTIENT = 0.0074
COEFFS5 = (8.0, -1.0, 8.0 / 63.0, -1.0 / 112.0)
CENTER5 = 15.0 * (-205.0 / 72.0)

C = 32
SX = 4
NY = 64
NZ = 128
ROWS = SX * NY
PART = NY // 2
CY = C * NY
MESH = pl.DeviceIdType.MESH
F32 = jnp.float32
BF16 = jnp.bfloat16
VMEM_LIMIT = 58 * 2**20


def coefficient(distance):
    out = np.zeros(distance.shape, np.float32)
    for reach in range(1, 5):
        out[distance == reach] = COEFFS5[reach - 1]
    return out


def stencil_tables():
    row = np.arange(ROWS)
    x, y = row // NY, row % NY
    dx, dy = x[:, None] - x[None, :], y[:, None] - y[None, :]
    same_x, same_y = (dx == 0), (dy == 0)
    plane = coefficient(np.abs(dx)) * same_y + coefficient(np.abs(dy)) * same_x
    plane = np.concatenate([plane, plane], axis=1)
    z = np.arange(NZ)
    line = coefficient(np.abs(z[:, None] - z[None, :]))
    line = np.concatenate([line, line], axis=0)
    halo_z = np.zeros((32, NZ), np.float32)
    pick = np.zeros((32, NZ), np.float32)
    for k in range(4):
        halo_z[k] = coefficient(z + 4 - k)
        halo_z[16 + k] = coefficient(NZ + k - z)
        pick[k, NZ - 4 + k] = 1.0
        pick[16 + k, k] = 1.0
    return [t.astype(ml_dtypes.bfloat16) for t in (plane, line, halo_z, pick)]


def dot(a, b):
    return jnp.dot(a, b, preferred_element_type=F32)


def dot_nt(a, b):
    return lax.dot_general(a, b, (((1,), (1,)), ((), ())), preferred_element_type=F32)


def dot_tn(a, b):
    return lax.dot_general(a, b, (((0,), (0,)), ((), ())), preferred_element_type=F32)


def split(values):
    high = values.astype(BF16)
    return high, (values - high.astype(F32)).astype(BF16)


def iota(shape, dim):
    return lax.broadcasted_iota(jnp.int32, shape, dim)


def place():
    gx, gy, gz = lax.axis_index("gx"), lax.axis_index("gy"), lax.axis_index("gz")
    slab = gx * 4 + gy

    def at(step_x, step_z):
        other = lax.rem(slab + 32 + step_x, 32)
        return (other // 4, lax.rem(other, 4), lax.rem(gz + 8 + step_z, 8))

    inside = {1: (slab < 31, gz < 7), -1: (slab > 0, gz > 0)}
    sides = {}
    for dx in (1, 0, -1):
        for dz in (0, 1, -1):
            if dx == 0 and dz == 0:
                continue
            present = None
            if dx:
                present = inside[dx][0]
            if dz:
                present = inside[dz][1] if present is None else present & inside[dz][1]
            sides[dx, dz] = (present, at(dx, dz))
    return slab, gz, sides


def column(rows, lane):
    picked = (iota((rows, NZ), 0) == 0) & (iota((rows, NZ), 1) == lane)
    return jnp.where(picked, 1.0, 0.0).astype(BF16)


def kernel(
    f_hbm, w_ref, v_ref, bias_ref, wave_hbm, born_hbm, adj_hbm, sx_ref, sy_ref, rx_ref, ry_ref,
    amp_ref, plane_t, line_t, halo_z_t, pick_t,
    born_out, adj_out, fg_out, weight_out,
    feats, band, wide, planes, rim_z, conv_x, conv_z, conv_c,
    waves, borns, drives, adjoint, duals, parts, base, halves, from_x, edges, from_z,
    stiff, stiff5, stiff_step, cot_scale, grad, spot, weight,
    cot, cot_edge, cot_z, cot_c, taps, moments, packed, slots, grads,
    in_sem, out_sem, sx_sem, rx_sem, sz_sem, rz_sem, sc_sem, rc_sem, sr_sem, rr_sem,
):
    slab, gz, sides = place()
    gx, gy = lax.axis_index("gx"), lax.axis_index("gy")
    loads = [
        pltpu.make_async_copy(f_hbm, feats, in_sem.at[0]),
        pltpu.make_async_copy(wave_hbm, waves.at[pl.ds(0, 2)], in_sem.at[1]),
        pltpu.make_async_copy(born_hbm, borns.at[pl.ds(0, 2)], in_sem.at[2]),
        pltpu.make_async_copy(adj_hbm, adjoint, in_sem.at[3]),
    ]
    for load in loads:
        load.start()

    def clear(side, writes):
        @pl.when(jnp.logical_not(sides[side][0]))
        def _():
            for ref in writes:
                ref[...] = jnp.zeros(ref.shape, ref.dtype)

    clear((-1, 0), [from_x.at[:, :, :, 0], conv_x.at[0], cot.at[pl.ds(0, NY)]])
    clear((1, 0), [from_x.at[:, :, :, 1], conv_x.at[1], cot.at[pl.ds(5 * NY, NY)]])
    clear((0, -1), [from_z.at[:, :, pl.ds(0, 16)], conv_z.at[0], cot_z.at[0]])
    clear((0, 1), [from_z.at[:, :, pl.ds(16, 16)], conv_z.at[1], cot_z.at[1]])
    for k, dz in enumerate((-1, 1)):
        for h, dx in enumerate((-1, 1)):
            clear((dx, dz), [conv_c.at[k, h], cot_c.at[k, h]])

    in_z = gz * 2 + lax.rem(gy, 2)
    in_x = gx * 2 + gy // 2
    groups = (
        (in_z, lambda k: (gx, gy // 2 * 2 + lax.rem(k, 2), k // 2)),
        (in_x, lambda k: (k // 2, lax.rem(k, 2) * 2 + lax.rem(gy, 2), gz)),
    )
    barrier = pltpu.get_barrier_semaphore()
    for present, device in sides.values():
        @pl.when(present)
        def _(device=device):
            pl.semaphore_signal(barrier, inc=1, device_id=device, device_id_type=MESH)
    for me, device in groups:
        for step in range(1, 16):
            pl.semaphore_signal(
                barrier, inc=1, device_id=device(lax.rem(me + step, 16)), device_id_type=MESH
            )

    def remote(src, dst, send, recv, device):
        return pltpu.make_async_remote_copy(
            src_ref=src, dst_ref=dst, send_sem=send, recv_sem=recv,
            device_id=device, device_id_type=MESH,
        )

    def start(exchange):
        for side, copy in exchange.items():
            @pl.when(sides[side][0])
            def _(copy=copy):
                copy.start()

    def arrive(exchange):
        for dx, dz in exchange:
            @pl.when(sides[dx, dz][0])
            def _(dx=dx, dz=dz):
                exchange[-dx, -dz].wait_recv()

    def leave(exchange):
        for side, copy in exchange.items():
            @pl.when(sides[side][0])
            def _(copy=copy):
                copy.wait_send()

    def finish(exchange):
        arrive(exchange)
        leave(exchange)

    def x_halo(par, f, h):
        high = halves.at[par, f, 0, :, pl.ds(h * PART, PART)]
        return {
            (dx, 0): remote(
                high, from_x.at[par, f, h, k],
                sx_sem.at[par, f, 2 * h + k], rx_sem.at[par, f, 2 * h + k], sides[dx, 0][1])
            for k, dx in enumerate((1, -1))
        }

    def z_halo(par, f):
        return {
            (0, dz): remote(
                edges.at[par, f, pl.ds(16 * k, 16)], from_z.at[par, f, pl.ds(16 * k, 16)],
                sz_sem.at[par, f, k], rz_sem.at[par, f, k], sides[0, dz][1])
            for k, dz in enumerate((1, -1))
        }

    def take(ref, at, h):
        return jnp.concatenate(
            [ref[(*at, pl.ds(x * NY + h * PART, PART))] for x in range(SX)], axis=0
        )

    def put(ref, at, h, values):
        for x in range(SX):
            ref[(*at, pl.ds(x * NY + h * PART, PART))] = values[x * PART : (x + 1) * PART]

    def send_x(par, f, h, values):
        halves[par, f, 0, :, pl.ds(h * PART, PART)] = values.astype(BF16).reshape(SX, PART, NZ)
        start(x_halo(par, f, h))

    def send_z(par, f):
        high = halves[par, f, 0].reshape(ROWS, NZ)
        edges[par, f] = dot_nt(pick_t[...], high).astype(BF16)
        start(z_halo(par, f))

    def inner(par, f, values):
        high = halves[par, f, 0].reshape(ROWS, NZ)
        low = (values - high.astype(F32)).astype(BF16)
        halves[par, f, 1] = low.reshape(SX, NY, NZ)
        part = dot(jnp.concatenate([high, low], axis=1), line_t[...])
        part = part + dot(plane_t[...], halves[par, f].reshape(2 * ROWS, NZ))
        return part + CENTER5 * values

    def outer_z(par, f):
        arrive(z_halo(par, f))
        return dot_tn(from_z[par, f], halo_z_t[...])

    def outer_x(par, f, h):
        arrive(x_halo(par, f, h))
        left, right = [
            [from_x[par, f, h, k, x].astype(F32) for x in range(SX)] for k in range(2)
        ]
        out = []
        for x in range(SX):
            total = None
            for reach in range(4, 0, -1):
                for there, have in ((x - reach + SX, left), (x + reach - SX, right)):
                    if 0 <= there < SX:
                        term = COEFFS5[reach - 1] * have[there]
                        total = term if total is None else total + term
            out.append(total)
        return jnp.concatenate(out, axis=0)

    def release(par, f):
        leave(z_halo(par, f))
        for h in range(2):
            leave(x_halo(par, f, h))

    repeat = jnp.where(iota((C, CY), 1) // NY == iota((C, CY), 0), 1.0, 0.0).astype(BF16)
    expanded = [dot_tn(w_ref[...], repeat), dot_tn(v_ref[...], repeat)]
    offset = lax.rem(iota((NY, NZ), 1), NY) - iota((NY, NZ), 0)
    hit = [offset == j - 1 for j in range(3)]
    for i in range(3):
        for l in range(3):
            for o in range(2):
                first = ((i * 3 + l) * 2 + o) * NY
                for at in range(0, CY, NZ):
                    block = jnp.zeros((NY, NZ), F32)
                    for j in range(3):
                        tap = (i * 3 + j) * 3 + l
                        block = jnp.where(hit[j], expanded[o][tap : tap + 1, at : at + NZ], block)
                    band[first : first + NY, at : at + NZ] = block.astype(BF16)
    wide[:, 0:NZ] = jnp.zeros((CY, NZ), BF16)
    wide[:, 5 * NZ : 6 * NZ] = jnp.zeros((CY, NZ), BF16)
    loads[0].wait()
    for x in range(SX):
        wide[:, (x + 1) * NZ : (x + 2) * NZ] = feats[:, x].reshape(CY, NZ)
    lanes = iota((2 * NY, NZ), 1)

    def generate(pair):
        total = None
        for i in range(3):
            first = 2 * pair + i - 1
            if first < 0 or first > 4:
                continue
            term = dot(
                band[i * 6 * NY : (i + 1) * 6 * NY, :], wide[:, first * NZ : (first + 2) * NZ]
            )
            total = term if total is None else total + term
        for half in range(2):
            at = 2 * pair + half
            part = total[:, half * NZ : (half + 1) * NZ]
            lower, middle, upper = [part[l * 2 * NY : (l + 1) * 2 * NY] for l in range(3)]
            plane = middle + jnp.where(lanes > 0, pltpu.roll(lower, 1, 1), 0.0)
            planes[at] = plane + jnp.where(lanes < NZ - 1, pltpu.roll(upper, NZ - 1, 1), 0.0)
            for k, edge, lane in ((0, lower, NZ - 1), (1, upper, 0)):
                high, low = split(edge)
                rim_z[k, at] = dot_nt(column(8, lane), high) + dot_nt(column(8, lane), low)

    rims = {}
    for k, dx in enumerate((1, -1)):
        rims[dx, 0] = remote(
            planes.at[5 if dx > 0 else 0], conv_x.at[k], sc_sem.at[k], rc_sem.at[k],
            sides[dx, 0][1])
        for h, dz in enumerate((1, -1)):
            n = 4 + 2 * h + k
            rims[dx, dz] = remote(
                rim_z.at[h, 5 if dx > 0 else 0], conv_c.at[h, k], sc_sem.at[n], rc_sem.at[n],
                sides[dx, dz][1])
    depths = {
        (0, dz): remote(
            rim_z.at[h, pl.ds(1, 4)], conv_z.at[h], sc_sem.at[2 + h], rc_sem.at[2 + h],
            sides[0, dz][1])
        for h, dz in enumerate((1, -1))
    }

    generate(0)
    generate(2)
    pl.semaphore_wait(
        barrier, 30 + sum(jnp.where(present, 1, 0) for present, _ in sides.values())
    )
    start(rims)
    generate(1)
    start(depths)
    loads[1].wait()
    loads[2].wait()
    loads[3].wait()
    for f in range(4):
        values = (waves if f < 2 else borns)[1, f % 2]
        for h in range(2):
            send_x(0, f, h, take(waves if f < 2 else borns, (1, f % 2), h))
        send_z(0, f)
        parts[f] = inner(0, f, values)

    row = iota((ROWS, NZ), 0)
    z = iota((ROWS, NZ), 1)
    top = jnp.where(gz == 0, 1.0, 0.0)
    for s in range(2):
        at = (sx_ref[s] - slab * SX) * NY + sy_ref[s]
        inside = (sx_ref[s] >= slab * SX) & (sx_ref[s] < slab * SX + SX)
        at = jnp.where(inside, at, -1)
        spot[s] = jnp.where((row == at) & (z == SRC_DEPTH), top, 0.0)
    cells = jnp.where(
        rx_ref[...] // SX == slab, lax.rem(rx_ref[...], SX) * NY + ry_ref[...], -1
    )
    hits = jnp.zeros((ROWS, NZ), F32)
    for k in range(8):
        hits = hits + jnp.where(row == cells[k : k + 1, :], 1.0, 0.0)
    counts = jnp.sum(hits, axis=1, keepdims=True)
    weight[...] = jnp.where(z == REC_DEPTH, counts * counts * top, 0.0)

    def unpack(edge, lane):
        high, low = split(edge)
        return dot_tn(high, column(8, lane)) + dot_tn(low, column(8, lane))

    finish({**rims, **depths})
    for x in range(SX):
        rows = slice(x * NY, (x + 1) * NY)
        both = planes[x + 1]
        for h, lane in ((0, 0), (1, NZ - 1)):
            both = both + unpack(conv_z[h, x], lane)
            if x == 0:
                both = both + unpack(conv_c[h, 0], lane)
            if x == SX - 1:
                both = both + unpack(conv_c[h, 1], lane)
        if x == 0:
            both = both + conv_x[0]
        if x == SX - 1:
            both = both + conv_x[1]
        sigma = jax.nn.sigmoid(both[0:NY] + bias_ref[0])
        velocity = 1.5 + 3.0 * sigma
        slope = 3.0 * sigma * (1.0 - sigma)
        velocity_step = slope * both[NY:]
        stiffness = QUOTIENT * velocity * velocity
        stiff[rows] = stiffness
        stiff5[rows] = 0.2 * stiffness
        stiff_step[rows] = 2.0 * QUOTIENT * velocity * velocity_step
        cot_scale[rows] = slope * (2.0 * QUOTIENT * velocity)

    for s in range(2):
        base[s] = 2.0 * waves[1, s] - waves[0, s] + amp_ref[0] * spot[s] + stiff5[...] * parts[s]
        base[2 + s] = 2.0 * borns[1, s] - borns[0, s] + stiff5[...] * parts[2 + s]

    def advance(n, par, last):
        for s in range(2):
            depth = outer_z(par, s)
            parts[s] += depth
            base[s] += stiff5[...] * depth
            rests = []
            for h in range(2):
                rests.append(outer_x(par, s, h))
                if not last:
                    ahead = take(base, (s,), h) + take(stiff5, (), h) * rests[h]
                    send_x(1 - par, s, h, ahead)
                    put(waves, (n + 2, s), h, ahead)
            if not last:
                send_z(1 - par, s)
            for h in range(2):
                drive = 0.2 * (take(parts, (s,), h) + rests[h])
                put(drives, (n, s), h, drive)
                more = take(base, (2 + s,), h) + take(stiff_step, (), h) * drive
                put(base, (2 + s,), h, more)
            if not last:
                ahead = waves[n + 2, s]
                part = inner(1 - par, s, ahead)
                parts[s] = part
                base[s] = (
                    2.0 * ahead - waves[n + 1, s] + amp_ref[n + 1] * spot[s] + stiff5[...] * part
                )
            release(par, s)
        for s in range(2):
            f = 2 + s
            base[f] += stiff5[...] * outer_z(par, f)
            for h in range(2):
                ahead = take(base, (f,), h) + take(stiff5, (), h) * outer_x(par, f, h)
                if not last:
                    send_x(1 - par, f, h, ahead)
                put(borns, (n + 2, s), h, ahead)
            if not last:
                send_z(1 - par, f)
                ahead = borns[n + 2, s]
                part = inner(1 - par, f, ahead)
                base[f] = 2.0 * ahead - borns[n + 1, s] + stiff5[...] * part
            release(par, f)

    def forward(n, carry):
        advance(n, lax.rem(n, 2), False)
        return carry

    lax.fori_loop(0, NT - 1, forward, 0)
    advance(NT - 1, (NT - 1) % 2, True)
    stores = [pltpu.make_async_copy(borns.at[pl.ds(NT, 2)], born_out, out_sem.at[0])]
    stores[0].start()

    def settle(n, s, newer, newest, part):
        duals[0, s] = newer
        duals[1, s] = newest
        base[4 + s] = 2.0 * newer - newest + weight[...] * borns[n, s] + 0.2 * part

    for s in range(2):
        newer = adjoint[1, s] + weight[...] * borns[NT + 1, s]
        parts[s] = newer
        for h in range(2):
            send_x(0, 4 + s, h, take(stiff, (), h) * take(parts, (s,), h))
        send_z(0, 4 + s)
        part = inner(0, 4 + s, stiff[...] * newer)
        settle(NT, s, newer, -adjoint[0, s], part)
    grad[...] = duals[0, 0] * drives[NT - 1, 0] + duals[0, 1] * drives[NT - 1, 1]

    def retreat(m, par):
        n = NT - 1 - m
        for s in range(2):
            f = 4 + s
            base[f] += 0.2 * outer_z(par, f)
            for h in range(2):
                current = take(base, (f,), h) + 0.2 * outer_x(par, f, h)
                send_x(1 - par, f, h, take(stiff, (), h) * current)
                put(parts, (s,), h, current)
            send_z(1 - par, f)
            current = parts[s]
            part = inner(1 - par, f, stiff[...] * current)
            grad[...] += current * drives[n - 1, s]
            settle(n, s, current, duals[0, s], part)
            release(par, f)

    def backward(m, carry):
        retreat(m, lax.rem(m, 2))
        return carry

    lax.fori_loop(0, NT - 1, backward, 0)

    cot[NY : 5 * NY] = (cot_scale[...] * grad[...]).astype(BF16)
    own = cot[NY : 5 * NY]
    edge_lane = jnp.where(iota((32, NZ), 0) == 0, NZ - 1, jnp.where(iota((32, NZ), 0) == 16, 0, -1))
    edge_pick = jnp.where(iota((32, NZ), 1) == edge_lane, 1.0, 0.0).astype(BF16)
    around = {}
    for k, dx in enumerate((1, -1)):
        around[dx, 0] = remote(
            cot.at[pl.ds(4 * NY if dx > 0 else NY, NY)],
            cot.at[pl.ds(0 if dx > 0 else 5 * NY, NY)],
            sc_sem.at[8 + k], rc_sem.at[8 + k], sides[dx, 0][1])
    for h, dz in enumerate((1, -1)):
        around[0, dz] = remote(
            cot_edge.at[pl.ds(16 * h, 16)], cot_z.at[h],
            sc_sem.at[10 + h], rc_sem.at[10 + h], sides[0, dz][1])
        for k, dx in enumerate((1, -1)):
            n = 12 + 2 * h + k
            around[dx, dz] = remote(
                cot_edge.at[pl.ds(16 * h, 16), pl.ds(2 * NY if dx > 0 else 0, 2 * NY)],
                cot_c.at[h, k], sc_sem.at[n], rc_sem.at[n], sides[dx, dz][1])
    cot_edge[...] = dot_nt(edge_pick, own).astype(BF16)
    start(around)

    span = 9 * NY
    il = iota((27, span), 1) // NY
    expanded = []
    for j in range(3):
        tap = (il // 3 * 3 + j) * 3 + lax.rem(il, 3)
        expanded.append(dot(w_ref[...], jnp.where(iota((27, span), 0) == tap, 1.0, 0.0).astype(BF16)))
    offset = iota((NY, span), 0) - lax.rem(iota((NY, span), 1), NY)
    for c in range(C):
        block = jnp.zeros((NY, span), F32)
        for j in range(3):
            block = jnp.where(offset == j - 1, expanded[j][c : c + 1, :], block)
        grads[c * NY : (c + 1) * NY, :] = block.astype(BF16)

    finish(around)
    lanes = iota((6 * NY, NZ), 1)
    whole = cot[...].astype(F32)
    shifted = {1: cot[...]}
    for l, h, lane, turn in ((0, 1, NZ - 1, NZ - 1), (2, 0, 0, 1)):
        inside = jnp.where(lanes == lane, 0.0, pltpu.roll(whole, turn, 1))
        pick = column(16, lane)
        rim = jnp.concatenate(
            [
                dot_tn(cot_c[h, 0], pick)[NY:],
                dot_tn(cot_z[h], pick),
                dot_tn(cot_c[h, 1], pick)[:NY],
            ],
            axis=0,
        )
        shifted[l] = (inside + rim).astype(BF16)
    for x in range(SX):
        for i in range(3):
            for l in range(3):
                at = (i * 3 + l) * NY
                first = (x - i + 2) * NY
                taps[x // 2, at : at + NY, (x % 2) * NZ : (x % 2 + 1) * NZ] = (
                    shifted[l][first : first + NY, :]
                )

    def moment_step(k, carry):
        first = pl.multiple_of(k * 8, 8)
        rows = pl.ds(pl.multiple_of(k * 8 * NY, 8 * NY), 8 * NY)
        total = dot_nt(wide[rows, NZ : 3 * NZ], taps[0]) + dot_nt(wide[rows, 3 * NZ : 5 * NZ], taps[1])
        total = total.reshape(8, NY, span)
        for j in range(3):
            part = jnp.where((offset == j - 1)[None], total, 0.0)
            moments[j, pl.ds(first, 8), :] = jnp.sum(part, axis=1)
        return carry

    lax.fori_loop(0, C // 8, moment_step, 0)
    il = iota((span, NZ), 0) // NY
    total = jnp.zeros((C, NZ), F32)
    for j in range(3):
        tap = (il // 3 * 3 + j) * 3 + lax.rem(il, 3)
        pick = jnp.where(iota((span, NZ), 1) == tap, 1.0, 0.0).astype(BF16)
        values = moments[j]
        for _ in range(3):
            high = values.astype(BF16)
            total = total + dot(high, pick)
            values = values - high.astype(F32)
    pack = total[0:8]
    for k in range(1, 4):
        pack = pack + pltpu.roll(total[8 * k : 8 * k + 8], 32 * k, 1)

    def feature_step(k, carry):
        first = pl.multiple_of(k * 8, 8)
        rows = pl.ds(pl.multiple_of(k * 8 * NY, 8 * NY), 8 * NY)
        for pair in range(2):
            product = dot(grads[rows, :], taps[pair]).astype(BF16)
            for half in range(2):
                feats[pl.ds(first, 8), 2 * pair + half] = product[
                    :, half * NZ : (half + 1) * NZ
                ].reshape(8, NY, NZ)
        return carry

    def finish_adjoint():
        for s in range(2):
            adjoint[0, s] = -duals[0, s]
            f, par = 4 + s, (NT - 1) % 2
            base[f] += 0.2 * outer_z(par, f) - weight[...] * borns[1, s]
            for h in range(2):
                put(adjoint, (1, s), h, take(base, (f,), h) + 0.2 * outer_x(par, f, h))
            release(par, f)
        stores.append(pltpu.make_async_copy(adjoint, adj_out, out_sem.at[1]))
        stores[-1].start()

    for g, (me, device) in enumerate(groups):
        packed[g] = pack
        slots[g, me] = pack
        copies = []
        for step in range(1, 16):
            copies.append(remote(
                packed.at[g], slots.at[g, me], sr_sem.at[g, step], rr_sem.at[g, me],
                device(lax.rem(me + step, 16)),
            ))
            copies[-1].start()
        if g == 0:
            finish_adjoint()
        lax.fori_loop(2 * g, 2 * g + 2, feature_step, 0)
        half = pl.ds(16 * g, 16)
        stores.append(pltpu.make_async_copy(feats.at[half], fg_out.at[half], out_sem.at[2 + g]))
        stores[-1].start()
        for step in range(1, 16):
            k = lax.rem(me + step, 16)
            remote(
                packed.at[g], slots.at[g, k], sr_sem.at[g, step], rr_sem.at[g, k], device(k)
            ).wait_recv()
        for copy in copies:
            copy.wait_send()
        pack = slots[g, 0]
        for k in range(1, 16):
            pack = pack + slots[g, k]
    scale = 1.0 / math.sqrt(ROWS * NZ * 256)
    for k in range(4):
        rows = slice(8 * k, 8 * k + 8)
        values = pltpu.roll(pack, NZ - 32 * k, 1) if k else pack
        weight_out[rows, :] = values[:, :27] * scale + v_ref[...][rows].astype(F32)
    for store in stores:
        store.wait()


def settle_kernel(*refs):
    ins, outs, bufs, sem_in, sem_out = refs[:4], refs[4:8], refs[8:12], refs[12], refs[13]
    pieces = [(3, pl.ds(0, C))]
    for n in (0, 1):
        pieces += [(n, pl.ds(k, 1)) for k in range(2)]
    pieces += [(2, pl.ds(8 * k, 8)) for k in range(4)]
    loads, stores = [], []
    for k, (n, part) in enumerate(pieces):
        loads.append(pltpu.make_async_copy(ins[n].at[part], bufs[n].at[part], sem_in.at[k]))
        stores.append(pltpu.make_async_copy(bufs[n].at[part], outs[n].at[part], sem_out.at[k]))
        loads[k].start()
    for load, store in zip(loads, stores):
        load.wait()
        store.start()
    for store in stores:
        store.wait()


def settle_call(*arrays):
    dma = pltpu.SemaphoreType.DMA
    return pl.pallas_call(
        settle_kernel,
        out_shape=[jax.ShapeDtypeStruct(a.shape, a.dtype) for a in arrays],
        in_specs=[pl.BlockSpec(memory_space=pl.ANY)] * 4,
        out_specs=[pl.BlockSpec(memory_space=pl.ANY)] * 4,
        scratch_shapes=[pltpu.VMEM(a.shape, a.dtype) for a in arrays] + [dma((9,)), dma((9,))],
        compiler_params=pltpu.CompilerParams(vmem_limit_bytes=VMEM_LIMIT),
    )(*arrays)


def shards(
    features, conv_weight, weight_step, conv_bias, wave_state, born_in, adjoint_in,
    shot_x, shot_y, rec_x, rec_y,
):
    steps = np.arange(NT, dtype=np.float64)
    spread = (0.45 * (steps - 5.0)) ** 2
    amplitude = (20.0 * (1.0 - 2.0 * spread) * np.exp(-spread)).astype(np.float32)
    hbm, vmem, smem = [
        pl.BlockSpec(memory_space=m) for m in (pl.ANY, pltpu.VMEM, pltpu.SMEM)
    ]
    field = (ROWS, NZ)
    pair = (2, *field)
    dma = pltpu.SemaphoreType.DMA
    born, adjoint, feature_grad, weight_product = pl.pallas_call(
        kernel,
        out_shape=(
            jax.ShapeDtypeStruct((2, *pair), F32),
            jax.ShapeDtypeStruct((2, *pair), F32),
            jax.ShapeDtypeStruct((C, SX, NY, NZ), BF16),
            jax.ShapeDtypeStruct((C, 27), F32),
        ),
        in_specs=[hbm, vmem, vmem, smem, hbm, hbm, hbm, smem, smem, vmem, vmem, smem] + [vmem] * 4,
        out_specs=[hbm, hbm, hbm, vmem],
        scratch_shapes=[
            pltpu.VMEM((C, SX, NY, NZ), BF16),
            pltpu.VMEM((18 * NY, CY), BF16),
            pltpu.VMEM((CY, 6 * NZ), BF16),
            pltpu.VMEM((6, 2 * NY, NZ), F32),
            pltpu.VMEM((2, 6, 8, 2 * NY), F32),
            pltpu.VMEM((2, 2 * NY, NZ), F32),
            pltpu.VMEM((2, 4, 8, 2 * NY), F32),
            pltpu.VMEM((2, 2, 8, 2 * NY), F32),
            pltpu.VMEM((NT + 2, *pair), F32),
            pltpu.VMEM((NT + 2, *pair), F32),
            pltpu.VMEM((NT, *pair), F32),
            pltpu.VMEM((2, *pair), F32),
            pltpu.VMEM((2, *pair), F32),
            pltpu.VMEM((4, *field), F32),
            pltpu.VMEM((6, *field), F32),
            pltpu.VMEM((2, 6, 2, SX, NY, NZ), BF16),
            pltpu.VMEM((2, 6, 2, 2, SX, PART, NZ), BF16),
            pltpu.VMEM((2, 6, 32, ROWS), BF16),
            pltpu.VMEM((2, 6, 32, ROWS), BF16),
            pltpu.VMEM(field, F32),
            pltpu.VMEM(field, F32),
            pltpu.VMEM(field, F32),
            pltpu.VMEM(field, F32),
            pltpu.VMEM(field, F32),
            pltpu.VMEM(pair, F32),
            pltpu.VMEM(field, F32),
            pltpu.VMEM((6 * NY, NZ), BF16),
            pltpu.VMEM((32, ROWS), BF16),
            pltpu.VMEM((2, 16, ROWS), BF16),
            pltpu.VMEM((2, 2, 16, 2 * NY), BF16),
            pltpu.VMEM((2, 9 * NY, 2 * NZ), BF16),
            pltpu.VMEM((3, C, 9 * NY), F32),
            pltpu.VMEM((2, 8, NZ), F32),
            pltpu.VMEM((2, 16, 8, NZ), F32),
            pltpu.VMEM((CY, 9 * NY), BF16),
            dma((4,)), dma((4,)),
            dma((2, 6, 4)), dma((2, 6, 4)), dma((2, 6, 2)), dma((2, 6, 2)),
            dma((16,)), dma((16,)), dma((2, 16)), dma((2, 16)),
        ],
        compiler_params=pltpu.CompilerParams(
            collective_id=0, has_side_effects=True, vmem_limit_bytes=VMEM_LIMIT
        ),
    )(
        features, conv_weight, weight_step, conv_bias,
        *[v.reshape(2, *pair) for v in (wave_state, born_in, adjoint_in)],
        shot_x, shot_y, rec_x.reshape(8, 128), rec_y.reshape(8, 128),
        jnp.asarray(amplitude), *[jnp.asarray(t) for t in stencil_tables()],
    )
    born, adjoint, feature_grad, weight_product = settle_call(
        born, adjoint, feature_grad, weight_product
    )
    shape = (2, 2, SX, NY, NZ)
    return born.reshape(shape), adjoint.reshape(shape), weight_product, feature_grad


def solution(mesh):
    grid = P(None, None, ("gx", "gy"), None, "gz")
    maps = P(None, ("gx", "gy"), None, "gz")
    return jax.shard_map(
        shards,
        mesh=mesh,
        in_specs=(maps, P(), P(), P(), grid, grid, grid, P(), P(), P(), P()),
        out_specs=(grid, grid, P(), maps),
        check_vma=False,
    )
```
